128 devices in a mesh: wide: 8 (over z, core), narrow: 16 (over y, x).
Axes of the slice: x: 4, y: 4, z: 4, core: 2. Of those that a mesh axis runs over, the one named last changes fastest.
Arguments:
- hidden_in: float32 [2, 64, 8192], P(None, None, 'narrow'), may hold values from -100 to 100
- attn_gain: float32 [8192], P('narrow'), may hold values from 0.1 to 1.9
- w_query: bfloat16 [8192, 8192], P('narrow', 'wide'), may hold values from -0.0625 to 0.0625
- w_key: bfloat16 [8192, 1024], P('narrow', 'wide'), may hold values from -0.0625 to 0.0625
- w_value: bfloat16 [8192, 1024], P('narrow', 'wide'), may hold values from -0.0625 to 0.0625
- w_out: bfloat16 [8192, 8192], P('wide', 'narrow'), may hold values from -0.0625 to 0.0625
- ffn_gain: float32 [8192], P('narrow'), may hold values from 0.1 to 1.9
- w_gate: bfloat16 [8192, 28672], P('narrow', 'wide'), may hold values from -0.0625 to 0.0625
- w_up: bfloat16 [8192, 28672], P('narrow', 'wide'), may hold values from -0.0625 to 0.0625
- w_down: bfloat16 [28672, 8192], P('wide', 'narrow'), may hold values from -0.03125 to 0.03125
- key_cache: bfloat16 [2, 64, 8, 2048, 128], P(None, 'narrow', 'wide'), may hold values from -256 to 256
- value_cache: bfloat16 [2, 64, 8, 2048, 128], P(None, 'narrow', 'wide'), may hold values from -6 to 6
- cache_len: int32 [2, 64], P(None, 'narrow'), may hold values from 1 to 2048, as said below
Outputs:
- hidden_out: float32 [2, 64, 8192], P(None, None, 'narrow')
The draws below stay inside these ranges and needn't reach their ends.
Inputs may be any that keep to these rules, and one draw needn't show every extreme that they name: `cache_len`: in every micro-batch one row's cache holds exactly 2048 tokens.
All inputs are finite; a program needn't handle non-finite values.
Results may differ from the reference program's by a relative error of at most 0.0086.
Values may be sent and summed in bfloat16 or wider, within the bound.
No kernel may reach another device: no remote copies, remote signals or barrier semaphores. Data moves between devices by JAX's collectives and lax.ppermute only.
A program may use at most 128 MiB of HBM per device.

```python
import math
import jax
import jax.numpy as jnp
from jax import lax

D = 8192
FF = 28672
QH = 64
KV = 8
HD = 128
MB = 2
CACHE = 2048
ROWS = 64


def draw_hidden_in(key, part):
    key = jax.random.fold_in(key, 1)
    first_key, second_key, third_key = jax.random.split(key, 3)
    base = jnp.clip(jax.random.normal(first_key, (MB, ROWS, D), jnp.float32), -6.0, 6.0)
    row_scale = jnp.exp(jax.random.uniform(second_key, (MB, ROWS, 1), jnp.float32, math.log(0.3), math.log(3.0)))
    column_scale = jnp.exp(jax.random.uniform(third_key, (1, 1, D), jnp.float32, math.log(0.4), math.log(2.5)))
    trend = 3.0 ** (jnp.arange(D, dtype=jnp.float32) / D - 0.5)
    return base * row_scale * column_scale * trend[None, None, :]


def draw_key_cache(key, part):
    key = jax.random.fold_in(key, 3)
    first_key = jax.random.fold_in(key, 0)
    shape = (MB, ROWS, KV, CACHE, HD)
    base = jnp.clip(jax.random.normal(first_key, shape, jnp.float32), -6.0, 6.0)
    return base.astype(jnp.bfloat16)


def draw_cache_len(key, part):
    key = jax.random.fold_in(key, 2)
    first_key, second_key, third_key = jax.random.split(key, 3)
    left = jax.random.randint(first_key, (MB, ROWS), 0, CACHE)
    right = jax.random.randint(second_key, (MB, ROWS), 0, CACHE)
    lengths = 1 + left * right // CACHE
    chosen = jax.random.randint(third_key, (MB, 1), 0, ROWS)
    lengths = jnp.where(jnp.arange(ROWS)[None, :] == chosen, CACHE, lengths)
    return lengths.astype(jnp.int32)


def block_levels(own_key, dims, cuts, low, top_value):
    def one(axis_at, shards_of):
        heights = jax.random.uniform(jax.random.fold_in(jax.random.fold_in(own_key, 6), axis_at), (shards_of,), jnp.float32, low / len(cuts), top_value / len(cuts))
        return jnp.repeat(jnp.exp(heights), dims[axis_at] // shards_of).reshape((-1,) + (1,) * (len(dims) - axis_at - 1))

    gain = one(*cuts[0])
    for cut in cuts[1:]:
        gain = gain * one(*cut)
    return gain


def noise(stream_key, shape, deviation, reach, pieces=(), kind=jnp.bfloat16):
    result = jax.random.normal(stream_key, shape, jnp.float32) * deviation
    if len(pieces) > 0:
        result = block_levels(stream_key, shape, pieces, -0.22, 0.18) * result
    return jnp.clip(result, min=-reach, max=reach).astype(kind)


def setup_inputs(seed: int = 0) -> dict:
    splits = jax.random.split(jax.random.key(seed), 14)
    hidden_in = draw_hidden_in(jax.random.fold_in(splits[13], 71), 0)
    attn_gain = jnp.clip(1.0 + 0.18 * jax.random.normal(splits[1], (D,), jnp.float32), 0.1, 1.9)
    w_query = noise(splits[2], (D, QH * HD), D ** -0.5, 0.0625, ((0, 16), (1, 8)))
    w_key = noise(splits[3], (D, KV * HD), D ** -0.5, 0.0625, ((0, 16), (1, 8)))
    w_value = noise(splits[4], (D, KV * HD), D ** -0.5, 0.0625, ((0, 16), (1, 8)))
    w_out = noise(splits[5], (QH * HD, D), (QH * HD) ** -0.5, 0.0625, ((0, 8), (1, 16)))
    ffn_gain = jnp.clip(1.0 + 0.18 * jax.random.normal(splits[6], (D,), jnp.float32), 0.1, 1.9)
    w_gate = noise(splits[7], (D, FF), D ** -0.5, 0.0625, ((0, 16), (1, 8)))
    w_up = noise(splits[8], (D, FF), D ** -0.5, 0.0625, ((0, 16), (1, 8)))
    w_down = noise(splits[9], (FF, D), FF ** -0.5, 0.03125, ((0, 8), (1, 16)))
    key_cache = draw_key_cache(jax.random.fold_in(splits[13], 71), 0)
    value_cache = noise(splits[11], (MB, ROWS, KV, CACHE, HD), 1.0, 6.0, ((1, 16), (2, 8)))
    cache_len = draw_cache_len(jax.random.fold_in(splits[13], 71), 0)
    return dict(hidden_in=hidden_in, attn_gain=attn_gain, w_query=w_query, w_key=w_key, w_value=w_value, w_out=w_out, ffn_gain=ffn_gain, w_gate=w_gate, w_up=w_up, w_down=w_down, key_cache=key_cache, value_cache=value_cache, cache_len=cache_len)


epsilon = 1e-05

def rotate(values, places):
    halfway = values.shape[-1] // 2
    angles_base = 500000.0 ** (-jnp.arange(halfway, dtype=jnp.float32) * 2.0 / values.shape[-1])
    angles = places * angles_base
    cosines = jnp.cos(angles)
    sinewave = jnp.sin(angles)
    lower_half = values[..., :halfway]
    upper_half = values[..., halfway:]
    return jnp.concatenate([lower_half * cosines - upper_half * sinewave, upper_half * cosines + lower_half * sinewave], axis=-1)

def attend(queries, key_new, value_new, key_rows, value_rows, length):
    scaling = queries.shape[-1] ** (-0.5)
    scores = jnp.einsum('kgd,kld->kgl', queries.astype(jnp.float32), key_rows.astype(jnp.float32)) * scaling
    visible = jnp.arange(key_rows.shape[1]) < length
    scores = jnp.where(visible, scores, -jnp.inf)
    own_score = jnp.einsum('kgd,kd->kg', queries.astype(jnp.float32), key_new.astype(jnp.float32)) * scaling
    highest = jnp.maximum(lax.optimization_barrier(jnp.max(scores, axis=-1)), own_score)
    shifted = jnp.exp(scores - highest[..., None])
    own_term = jnp.exp(own_score - highest)
    totals = lax.optimization_barrier(jnp.sum(shifted, axis=-1)) + own_term
    weights = (shifted / totals[..., None]).astype(jnp.bfloat16)
    own_weight = (own_term / totals).astype(jnp.bfloat16)
    attended = jnp.einsum('kgl,kld->kgd', weights.astype(jnp.float32), value_rows.astype(jnp.float32))
    attended = attended + own_weight.astype(jnp.float32)[..., None] * value_new.astype(jnp.float32)[:, None, :]
    return attended.astype(jnp.bfloat16)

def reference(hidden_in, attn_gain, w_query, w_key, w_value, w_out, ffn_gain, w_gate, w_up, w_down, key_cache, value_cache, cache_len):
    results = []
    for micro_index in range(MB):
        stream = hidden_in[micro_index]
        factor = lax.rsqrt(lax.optimization_barrier(jnp.sum(stream * stream, axis=-1)) / D + epsilon)[:, None]
        normed = (stream * attn_gain).astype(jnp.bfloat16)
        query_sum = jnp.dot(normed, w_query, preferred_element_type=jnp.float32) * factor
        key_sum = jnp.dot(normed, w_key, preferred_element_type=jnp.float32) * factor
        value_sum = jnp.dot(normed, w_value, preferred_element_type=jnp.float32) * factor
        places = cache_len[micro_index].astype(jnp.float32)[:, None, None]
        queries = rotate(query_sum.reshape(ROWS, QH, HD), places).astype(jnp.bfloat16)
        keys_new = rotate(key_sum.reshape(ROWS, KV, HD), places).astype(jnp.bfloat16)
        values_new = value_sum.reshape(ROWS, KV, HD).astype(jnp.bfloat16)
        queries = queries.reshape(ROWS, KV, QH // KV, HD)

        def one_row(packed):
            return attend(*packed)
        attended = lax.map(one_row, (queries, keys_new, values_new, key_cache[micro_index], value_cache[micro_index], cache_len[micro_index]))
        attended = attended.reshape(ROWS, QH * HD)
        middle = stream + jnp.dot(attended, w_out, preferred_element_type=jnp.float32)
        factor_two = lax.rsqrt(lax.optimization_barrier(jnp.sum(middle * middle, axis=-1)) / D + epsilon)[:, None]
        normed_two = (middle * ffn_gain).astype(jnp.bfloat16)
        gate_sum = jnp.dot(normed_two, w_gate, preferred_element_type=jnp.float32) * factor_two
        up_sum = jnp.dot(normed_two, w_up, preferred_element_type=jnp.float32) * factor_two
        hidden = (jax.nn.silu(gate_sum) * up_sum).astype(jnp.bfloat16)
        results.append(middle + jnp.dot(hidden, w_down, preferred_element_type=jnp.float32))
    return jnp.stack(results)
```

```python
import jax
import jax.numpy as jnp
from jax import lax
from jax.sharding import PartitionSpec as P

D = 8192
EPSILON = 1e-05
BF16 = jnp.bfloat16
F32 = jnp.float32


def swap_core():
    return [(z * 2 + c, z * 2 + 1 - c) for z in range(4) for c in range(2)]


def swap_z(partner):
    return [(z * 2 + c, partner[z] * 2 + c) for z in range(4) for c in range(2)]


STEPS = (swap_core(), swap_z((1, 0, 3, 2)), swap_z((3, 2, 1, 0)))


def rounded(values):
    return lax.reduce_precision(values, 8, 7)


def sum_wide(total):
    for pairs in STEPS:
        mine = rounded(total)
        other = lax.ppermute(mine.astype(BF16), "wide", pairs)
        total = mine + other.astype(F32)
    return total


def split_squares(squares, width):
    high = rounded(squares)
    low = squares - high
    lane = lax.broadcasted_iota(jnp.int32, (squares.shape[0], width), 1)
    return jnp.where(lane == 0, high[:, None], jnp.where(lane == 1, low[:, None], 0.0)).astype(BF16)


def exchange(payload):
    return lax.all_to_all(payload, "narrow", 0, 0, tiled=True)


def rotate(values, places):
    halfway = values.shape[-1] // 2
    angles_base = 500000.0 ** (-jnp.arange(halfway, dtype=F32) * 2.0 / values.shape[-1])
    angles = places * angles_base
    cosines = jnp.cos(angles)
    sinewave = jnp.sin(angles)
    a = values[..., :halfway]
    b = values[..., halfway:]
    return jnp.concatenate([a * cosines - b * sinewave, b * cosines + a * sinewave], axis=-1)


def body(
    hidden_in,
    attn_gain,
    w_query,
    w_key,
    w_value,
    w_out,
    ffn_gain,
    w_gate,
    w_up,
    w_down,
    key_cache,
    value_cache,
    cache_len,
):
    micro, _, width = hidden_in.shape
    rows = key_cache.shape[1]
    here = micro * rows
    parts = 16
    head = 128
    stream = hidden_in.reshape(micro, parts, rows, width).transpose(1, 0, 2, 3).reshape(-1, width)
    squares = jnp.sum(stream * stream, axis=-1)
    normed = (stream * attn_gain).astype(BF16)
    sums = [jnp.dot(normed, w, preferred_element_type=F32).astype(BF16) for w in (w_query, w_key, w_value)]
    payload = jnp.concatenate(sums + [split_squares(squares, head)], axis=-1)
    got = exchange(payload.reshape(parts, here, -1)).astype(F32).sum(axis=0)
    heads = w_query.shape[1] // head
    factor = lax.rsqrt((got[:, -head] + got[:, -head + 1]) / D + EPSILON)[:, None]
    lengths = cache_len.reshape(here)
    places = lengths.astype(F32)[:, None, None]
    split = heads * head
    queries = rotate((got[:, :split] * factor).reshape(here, heads, head), places).astype(BF16)
    key_new = rotate((got[:, split : split + head] * factor).reshape(here, 1, head), places).astype(BF16)
    value_new = (got[:, split + head : split + 2 * head] * factor).astype(BF16)

    keys = key_cache.reshape(here, -1, head)
    values = value_cache.reshape(here, -1, head)
    scaling = head ** (-0.5)
    scores = jnp.einsum("rgd,rld->rgl", queries, keys, preferred_element_type=F32) * scaling
    visible = jnp.arange(keys.shape[1])[None, None, :] < lengths[:, None, None]
    scores = jnp.where(visible, scores, -jnp.inf)
    own = jnp.sum(queries.astype(F32) * key_new.astype(F32), axis=-1) * scaling
    highest = jnp.maximum(jnp.max(scores, axis=-1), own)
    shifted = jnp.exp(scores - highest[..., None])
    own_term = jnp.exp(own - highest)
    totals = jnp.sum(shifted, axis=-1) + own_term
    weights = (shifted / totals[..., None]).astype(BF16)
    own_weight = rounded(own_term / totals)
    attended = jnp.einsum("rgl,rld->rgd", weights, values, preferred_element_type=F32)
    attended = attended + own_weight[..., None] * value_new.astype(F32)[:, None, :]
    attended = attended.astype(BF16).reshape(here, split)

    all_attended = exchange(jnp.broadcast_to(attended[None], (parts, here, split)))
    middle = stream + sum_wide(
        jnp.dot(all_attended.reshape(-1, split), w_out, preferred_element_type=F32)
    )
    squares_two = jnp.sum(middle * middle, axis=-1)
    normed_two = (middle * ffn_gain).astype(BF16)
    units = w_gate.shape[1]
    sums = [jnp.dot(normed_two, w, preferred_element_type=F32).astype(BF16) for w in (w_gate, w_up)]
    payload = jnp.concatenate(sums + [split_squares(squares_two, head)], axis=-1)
    got = exchange(payload.reshape(parts, here, -1)).astype(F32).sum(axis=0)
    factor_two = lax.rsqrt((got[:, -head] + got[:, -head + 1]) / D + EPSILON)[:, None]
    hidden = jax.nn.silu(got[:, :units] * factor_two) * (got[:, units : 2 * units] * factor_two)
    hidden = hidden.astype(BF16)
    all_hidden = exchange(jnp.broadcast_to(hidden[None], (parts, here, units)))
    result = middle + sum_wide(
        jnp.dot(all_hidden.reshape(-1, units), w_down, preferred_element_type=F32)
    )
    return result.reshape(parts, micro, rows, width).transpose(1, 0, 2, 3).reshape(hidden_in.shape)


def solution(mesh):
    return jax.shard_map(
        body,
        mesh=mesh,
        in_specs=(
            P(None, None, "narrow"),
            P("narrow"),
            P("narrow", "wide"),
            P("narrow", "wide"),
            P("narrow", "wide"),
            P("wide", "narrow"),
            P("narrow"),
            P("narrow", "wide"),
            P("narrow", "wide"),
            P("wide", "narrow"),
            P(None, "narrow", "wide", None, None),
            P(None, "narrow", "wide", None, None),
            P(None, "narrow"),
        ),
        out_specs=P(None, None, "narrow"),
        check_vma=False,
    )
```

```python
import functools

import jax
import jax.numpy as jnp
from jax import lax
from jax.experimental import pallas as pl
from jax.experimental.pallas import tpu as pltpu
from jax.sharding import PartitionSpec as P

D = 8192
EPSILON = 1e-05
BF16 = jnp.bfloat16
F32 = jnp.float32
SIDE = 4
PARTS = SIDE * SIDE
HEAD = 128
LANES = 128
VMEM = pl.BlockSpec(memory_space=pltpu.VMEM)
HBM = pl.BlockSpec(memory_space=pltpu.HBM)
SMEM = pl.BlockSpec(memory_space=pltpu.SMEM)
KIB = 1 << 10
MIB = 1 << 20


def wide_pairs(target):
    pairs = []
    for z in range(SIDE):
        for c in range(2):
            to_z, to_c = target(z, c)
            pairs.append((z * 2 + c, to_z % SIDE * 2 + to_c))
    return pairs


CORE_SWAP = wide_pairs(lambda z, c: (z, 1 - c))
NEXT_Z = wide_pairs(lambda z, c: (z + 1 if c == 0 else z - 1, c))
FAR_Z = wide_pairs(lambda z, c: (z + 2, c))


def plane_pairs(step, stage):
    pairs = []
    for w in range(2 * SIDE):
        for y in range(SIDE):
            for x in range(SIDE):
                along_x = (w % 2 == 0) == (stage == 0)
                to_y, to_x = (y, (x + step) % SIDE) if along_x else ((y + step) % SIDE, x)
                pairs.append((w * PARTS + y * SIDE + x, w * PARTS + to_y * SIDE + to_x))
    return pairs


def call(kernel, outs, limit, *operands, scratch=(), scalars=0, far=0, held=0):
    near = len(operands) - far
    specs = [SMEM] * scalars + [VMEM] * (near - scalars) + [HBM] * far
    size = sum(o.size * o.dtype.itemsize for o in operands)
    places = [None] * (near - held) + [pltpu.VMEM] * held + [pltpu.HBM] * far
    operands = [
        o if place is None else pltpu.with_memory_space_constraint(o, place)
        for o, place in zip(operands, places)
    ]
    return pl.pallas_call(
        kernel,
        out_shape=[jax.ShapeDtypeStruct(shape, kind) for shape, kind in outs],
        in_specs=specs,
        out_specs=[VMEM] * len(outs),
        scratch_shapes=scratch,
        compiler_params=pltpu.CompilerParams(vmem_limit_bytes=limit),
        cost_estimate=pl.CostEstimate(flops=0, bytes_accessed=size, transcendentals=0),
    )(*operands)


def place_squares(squares):
    high = squares.astype(BF16).astype(F32)
    low = squares - high
    lane = lax.broadcasted_iota(jnp.int32, (squares.shape[0], LANES), 1)
    return jnp.where(lane == 0, high, jnp.where(lane == 1, low, 0.0))


def project_kernel(
    len_ref, blocks_ref, core_ref, cos_ref, sin_ref, x_hbm, gain_hbm, wq_hbm, wk_hbm, wv_hbm, out_ref, stream_ref, x_ref, gain_ref, wq_ref, wk_ref,
    wv_ref, sems,
):
    pairs = ((x_hbm, x_ref), (gain_hbm, gain_ref), (wq_hbm, wq_ref), (wk_hbm, wk_ref), (wv_hbm, wv_ref))
    copies = [pltpu.make_async_copy(a, b, sems.at[i]) for i, (a, b) in enumerate(pairs)]
    for copy in copies:
        copy.start()
    copies[0].wait()
    copies[1].wait()
    rows = x_ref.shape[1] // PARTS
    for n in range(PARTS):
        for m in range(2):
            stream_ref[pl.ds((n * 2 + m) * rows, rows), :] = x_ref[m, pl.ds(n * rows, rows), :]
    stream = stream_ref[...]
    squares = jnp.sum(stream * stream, axis=-1, keepdims=True)
    normed = (stream * gain_ref[...]).astype(BF16)
    at = 0
    for copy, w_ref, exact in zip(copies[2:], (wq_ref, wk_ref, wv_ref), (True, True, False)):
        copy.wait()
        width = w_ref.shape[1]
        product = jnp.dot(normed, w_ref[...], preferred_element_type=F32)
        high = product.astype(BF16)
        out_ref[:, pl.ds(at, width)] = high
        at += width
        if exact:
            out_ref[:, pl.ds(at, width)] = (product - high.astype(F32)).astype(BF16)
            at += width
    out_ref[:, pl.ds(at, LANES)] = place_squares(squares).astype(out_ref.dtype)


def total_kernel(core_ref, mine_ref, other_ref, total_ref, half_ref):
    total = (mine_ref[...] + other_ref[...]).astype(BF16)
    total_ref[...] = total
    half = half_ref.shape[0]
    half_ref[...] = jnp.where(core_ref[0] == 0, total[:half, :], total[half:, :])


def pack_kernel(near_ref, far_ref, out_ref):
    rows = near_ref.shape[0]
    out_ref[pl.ds(0, rows), :] = near_ref[...]
    out_ref[pl.ds(rows, far_ref.shape[0]), :] = far_ref[...]


def attend_kernel(
    len_ref, got_ref, cos_ref, sin_ref, keys_hbm, values_hbm, out_ref, q_s, a_s, s_s, keys_s, values_s,
    key_sems, value_sems,
):
    here = got_ref.shape[1]
    cache = keys_s.shape[1]
    chunk = 512
    counts = [(len_ref[r] + chunk - 1) // chunk for r in range(here)]

    def fetch(far, near, sems, r, j):
        part = pl.ds(pl.multiple_of(j * chunk, chunk), chunk)
        return pltpu.make_async_copy(far.at[r, part], near.at[r, part], sems.at[r, j])

    def start(far, near, sems, r):
        @pl.loop(0, counts[r])
        def _(j):
            fetch(far, near, sems, r, j).start()

    def finish(far, near, sems, r):
        @pl.loop(0, counts[r])
        def _(j):
            fetch(far, near, sems, r, j).wait()

    for r in range(here):
        start(keys_hbm, keys_s, key_sems, r)
    for r in range(here):
        start(values_hbm, values_s, value_sems, r)
    for r in range(here):

        @pl.loop(counts[r], cache // chunk)
        def _(j):
            part = pl.ds(pl.multiple_of(j * chunk, chunk), chunk)
            values_s[r, part, :] = jnp.zeros((chunk, HEAD), BF16)

    total = got_ref[0].astype(F32)
    for n in range(1, PARTS):
        total = total + got_ref[n].astype(F32)
    heads = out_ref.shape[2] // HEAD
    split = heads * HEAD
    query = total[:, :split] + total[:, split : 2 * split]
    total = total[:, 2 * split :]
    squares = jnp.sum(total[:, 3 * HEAD :], axis=-1, keepdims=True)
    factor = lax.rsqrt(squares / D + EPSILON)
    cos, sin = cos_ref[...], sin_ref[...]

    def turned(part):
        part = part * factor
        return (part * cos + pltpu.roll(part, HEAD // 2, 1) * sin).astype(BF16).astype(F32)

    key_new = turned(total[:, :HEAD] + total[:, HEAD : 2 * HEAD])
    value_new = (total[:, 2 * HEAD : 3 * HEAD] * factor).astype(BF16).astype(F32)
    for h in range(heads):
        q_s[:, h, :] = turned(query[:, h * HEAD : (h + 1) * HEAD])
    scaling = HEAD ** (-0.5)
    position = lax.broadcasted_iota(jnp.int32, (1, cache), 1)
    for r in range(here):
        finish(keys_hbm, keys_s, key_sems, r)
    own = []
    for r in range(here):
        queries = q_s[r]
        scores = lax.dot_general(
            queries.astype(BF16),
            keys_s[r],
            (((1,), (1,)), ((), ())),
            preferred_element_type=F32,
        )
        s_s[pl.ds(r * heads, heads), :] = jnp.where(
            position < len_ref[r], scores * scaling, -jnp.inf
        )
        own.append(jnp.sum(queries * key_new[r : r + 1, :], axis=-1, keepdims=True) * scaling)
    weights, own_weights = [], []
    for r in range(here):
        scores = s_s[pl.ds(r * heads, heads), :]
        highest = jnp.maximum(jnp.max(scores, axis=-1, keepdims=True), own[r])
        shifted = jnp.exp(scores - highest)
        own_term = jnp.exp(own[r] - highest)
        totals = jnp.sum(shifted, axis=-1, keepdims=True) + own_term
        weights.append((shifted / totals).astype(BF16))
        own_weights.append((own_term / totals).astype(BF16).astype(F32))
    for r in range(here):
        finish(values_hbm, values_s, value_sems, r)
    for r in range(here):
        attended = jnp.dot(weights[r], values_s[r], preferred_element_type=F32)
        a_s[r] = attended + own_weights[r] * value_new[r : r + 1, :]
    for h in range(heads):
        part = a_s[:, h, :].astype(BF16)
        for n in range(PARTS):
            out_ref[n, :, pl.ds(h * HEAD, HEAD)] = part


def wide_total(refs):
    core_ref, mine_ref, near_ref, far_ref, other_ref = refs
    half = far_ref.shape[0]
    rows = mine_ref.shape[0]
    first = core_ref[0] == 0
    far, far_other = far_ref[...].astype(F32), other_ref[pl.ds(rows, half), :].astype(F32)
    opposite = jnp.concatenate(
        [jnp.where(first, far, far_other), jnp.where(first, far_other, far)], axis=0
    )
    sides = near_ref[...].astype(F32) + other_ref[pl.ds(0, rows), :].astype(F32)
    return (mine_ref[...].astype(F32) + opposite) + sides


def gate_kernel(
    core_ref, blocks_ref, mine_ref, near_ref, far_ref, other_ref, stream_ref, gain_ref, wg_ref,
    wu_ref, middle_ref, out0_ref, out1_ref, out2_ref, out3_ref, sorted_s, normed_s,
):
    middle_ref[...] = stream_ref[...] + wide_total(
        (core_ref, mine_ref, near_ref, far_ref, other_ref)
    )
    rows = middle_ref.shape[0] // PARTS
    for i in range(PARTS):
        start = pl.multiple_of(blocks_ref[i] * rows, rows)
        sorted_s[pl.ds(i * rows, rows), :] = middle_ref[pl.ds(start, rows), :]
    middle = sorted_s[...]
    squares = place_squares(jnp.sum(middle * middle, axis=-1, keepdims=True))
    normed_s[...] = (middle * gain_ref[...]).astype(BF16)
    outs = (out0_ref, out1_ref, out2_ref, out3_ref)
    units = wg_ref.shape[1]
    group = middle.shape[0] // SIDE
    tile = 512
    normed = normed_s[...]
    for at, w_ref in ((0, wg_ref), (units, wu_ref)):
        for j in range(0, units, tile):
            product = jnp.dot(normed, w_ref[:, pl.ds(j, tile)], preferred_element_type=F32)
            for d in range(SIDE):
                part = product[d * group : (d + 1) * group, :]
                outs[d][:, pl.ds(at + j, tile)] = part.astype(outs[d].dtype)
    for d in range(SIDE):
        part = squares[d * group : (d + 1) * group, :]
        outs[d][:, pl.ds(2 * units, LANES)] = part.astype(outs[d].dtype)


def middle_sum_kernel(a_ref, b_ref, c_ref, d_ref, own_ref, out1_ref, out2_ref, out3_ref):
    width = a_ref.shape[1]
    last = width - LANES
    tile = 1024
    rows = a_ref.shape[0] // SIDE

    def total(at, size):
        parts = [ref[:, pl.ds(at, size)].astype(F32) for ref in (a_ref, b_ref, c_ref, d_ref)]
        return (parts[0] + parts[1]) + (parts[2] + parts[3])

    outs = (own_ref, out1_ref, out2_ref, out3_ref)

    def put(at, size, value):
        for k in range(SIDE):
            outs[k][:, pl.ds(at, size)] = value[k * rows : (k + 1) * rows, :].astype(outs[k].dtype)

    for at in range(0, last, tile):
        put(at, tile, total(at, tile))
    put(last, LANES, place_squares(jnp.sum(total(last, LANES), axis=-1, keepdims=True)))


def hidden_kernel(a_ref, b_ref, c_ref, d_ref, out_ref):
    units = out_ref.shape[2]
    tile = 512

    def total(at, size):
        parts = [ref[:, pl.ds(at, size)].astype(F32) for ref in (a_ref, b_ref, c_ref, d_ref)]
        return (parts[0] + parts[1]) + (parts[2] + parts[3])

    squares = jnp.sum(total(2 * units, LANES), axis=-1, keepdims=True)
    factor = lax.rsqrt(squares / D + EPSILON)
    for at in range(0, units, tile):
        gate = total(at, tile) * factor
        up = total(units + at, tile) * factor
        hidden = (gate / (1.0 + jnp.exp(-gate)) * up).astype(BF16)
        for n in range(PARTS):
            out_ref[n, :, pl.ds(at, tile)] = hidden


def finish_kernel(core_ref, mine_ref, near_ref, far_ref, other_ref, middle_ref, out_ref):
    result = middle_ref[...] + wide_total((core_ref, mine_ref, near_ref, far_ref, other_ref))
    rows = out_ref.shape[1] // PARTS
    for n in range(PARTS):
        for m in range(2):
            at = (n * 2 + m) * rows
            out_ref[m, pl.ds(n * rows, rows), :] = result[at : at + rows, :]


def exchange(payload):
    return lax.all_to_all(payload, "narrow", 0, 0, tiled=True)


def sum_wide_parts(partial, core_flag):
    rows, width = partial.shape
    half = rows // 2
    mine, part = call(
        total_kernel,
        [((rows, width), BF16), ((half, width), BF16)],
        4 * MIB,
        core_flag,
        partial,
        lax.ppermute(partial, "wide", CORE_SWAP),
        scalars=1,
    )
    near = lax.ppermute(mine, "wide", NEXT_Z)
    far = lax.ppermute(part, "wide", FAR_Z)
    (both,) = call(pack_kernel, [((rows + half, width), BF16)], 4 * MIB, near, far)
    other = lax.ppermute(both, "wide", CORE_SWAP)
    return mine, near, far, other


def body(
    hidden_in,
    attn_gain,
    w_query,
    w_key,
    w_value,
    w_out,
    ffn_gain,
    w_gate,
    w_up,
    w_down,
    key_cache,
    value_cache,
    cache_len,
):
    micro, _, width = hidden_in.shape
    rows = key_cache.shape[1]
    here = micro * rows
    every = here * PARTS
    split = w_query.shape[1]
    units = w_gate.shape[1]
    core = lax.axis_index("wide") % 2
    at_y, at_x = lax.axis_index("narrow") // SIDE, lax.axis_index("narrow") % SIDE
    first, second = jnp.arange(PARTS) // SIDE, jnp.arange(PARTS) % SIDE
    step_y = jnp.where(core == 0, second, first)
    step_x = jnp.where(core == 0, first, second)
    blocks = ((at_y + step_y) % SIDE * SIDE + (at_x + step_x) % SIDE).astype(jnp.int32)
    core_flag = core.astype(jnp.int32)[None]

    lengths = cache_len.reshape(here)
    half = HEAD // 2
    base = 500000.0 ** (-jnp.arange(half, dtype=F32) * 2.0 / HEAD)
    angles = lengths.astype(F32)[:, None] * base[None]
    cosines, sines = jnp.cos(angles), jnp.sin(angles)
    cosines = jnp.concatenate([cosines, cosines], axis=-1)
    sines = jnp.concatenate([-sines, sines], axis=-1)

    payload, stream = call(
        project_kernel,
        [((every, 2 * split + 4 * HEAD), BF16), ((every, width), F32)],
        8 * MIB,
        lengths,
        blocks,
        core_flag,
        cosines,
        sines,
        hidden_in,
        attn_gain[None],
        w_query,
        w_key,
        w_value,
        scalars=3,
        far=5,
        scratch=[pltpu.VMEM(hidden_in.shape, F32), pltpu.VMEM((1, width), F32)]
        + [pltpu.VMEM(w.shape, BF16) for w in (w_query, w_key, w_value)]
        + [pltpu.SemaphoreType.DMA((5,))],
    )
    got = exchange(payload.reshape(PARTS, here, -1))

    (attended,) = call(
        attend_kernel,
        [((PARTS, here, split), BF16)],
        16 * MIB,
        lengths,
        got,
        cosines,
        sines,
        key_cache.reshape(here, -1, HEAD),
        value_cache.reshape(here, -1, HEAD),
        scalars=1,
        far=2,
        scratch=[pltpu.VMEM((here, split // HEAD, HEAD), F32)] * 2
        + [pltpu.VMEM((here * split // HEAD, key_cache.shape[3]), F32)]
        + [pltpu.VMEM((here, key_cache.shape[3], HEAD), BF16)] * 2
        + [pltpu.SemaphoreType.DMA((here, key_cache.shape[3] // 512))] * 2,
    )
    gathered = exchange(attended).reshape(every, split)
    parts = sum_wide_parts(jnp.dot(gathered, w_out, preferred_element_type=F32), core_flag)
    group = every // SIDE
    full = 2 * units + LANES
    middle, own, *sends = call(
        gate_kernel,
        [((every, width), F32), ((group, full), F32)] + [((group, full), BF16)] * (SIDE - 1),
        8 * MIB,
        core_flag,
        blocks,
        *parts,
        stream,
        ffn_gain[None],
        w_gate,
        w_up,
        scalars=2,
        held=2,
        scratch=[pltpu.VMEM((every, width), F32), pltpu.VMEM((every, width), BF16)],
    )
    axes = ("wide", "narrow")
    taken = {}
    for step in (1, 3, 2):
        taken[step] = lax.ppermute(sends[step - 1], axes, plane_pairs(step, 0))
    own, *sends = call(
        middle_sum_kernel,
        [((here, full), F32)] + [((here, full), BF16)] * (SIDE - 1),
        8 * MIB,
        own,
        taken[1],
        taken[2],
        taken[3],
    )
    for step in (1, 3, 2):
        taken[step] = lax.ppermute(sends[step - 1], axes, plane_pairs(step, 1))
    (hidden,) = call(
        hidden_kernel, [((PARTS, here, units), BF16)], 8 * MIB, own, taken[1], taken[2], taken[3]
    )
    gathered = exchange(hidden).reshape(every, units)
    parts = sum_wide_parts(jnp.dot(gathered, w_down, preferred_element_type=F32), core_flag)
    (result,) = call(
        finish_kernel, [(hidden_in.shape, F32)], 8 * MIB, core_flag, *parts, middle, scalars=1
    )
    return result


def solution(mesh):
    return jax.shard_map(
        body,
        mesh=mesh,
        in_specs=(
            P(None, None, "narrow"),
            P("narrow"),
            P("narrow", "wide"),
            P("narrow", "wide"),
            P("narrow", "wide"),
            P("wide", "narrow"),
            P("narrow"),
            P("narrow", "wide"),
            P("narrow", "wide"),
            P("wide", "narrow"),
            P(None, "narrow", "wide", None, None),
            P(None, "narrow", "wide", None, None),
            P(None, "narrow"),
        ),
        out_specs=P(None, None, "narrow"),
        check_vma=False,
    )
```

```python
import functools

import jax
import jax.numpy as jnp
from jax import lax
from jax.experimental import pallas as pl
from jax.experimental.pallas import tpu as pltpu
from jax.sharding import PartitionSpec as P

D = 8192
EPSILON = 1e-05
BF16 = jnp.bfloat16
F16 = jnp.float16
F32 = jnp.float32
SIDE = 4
PARTS = SIDE * SIDE
HEAD = 128
LANES = 128
VMEM = pl.BlockSpec(memory_space=pltpu.VMEM)
HBM = pl.BlockSpec(memory_space=pltpu.HBM)
SMEM = pl.BlockSpec(memory_space=pltpu.SMEM)
KIB = 1 << 10
MIB = 1 << 20
REACH = 8192.0
NORM_SCALES = (2.0**-2, 2.0**6, 2.0**16)


def wide_pairs(target):
    pairs = []
    for z in range(SIDE):
        for c in range(2):
            to_z, to_c = target(z, c)
            pairs.append((z * 2 + c, to_z % SIDE * 2 + to_c))
    return pairs


CORE_SWAP = wide_pairs(lambda z, c: (z, 1 - c))
NEXT_Z = wide_pairs(lambda z, c: (z + 1 if c == 0 else z - 1, c))
FAR_Z = wide_pairs(lambda z, c: (z + 2, c))


def plane_pairs(step, stage):
    pairs = []
    for w in range(2 * SIDE):
        for y in range(SIDE):
            for x in range(SIDE):
                along_x = (w % 2 == 0) == (stage == 0)
                to_y, to_x = (y, (x + step) % SIDE) if along_x else ((y + step) % SIDE, x)
                pairs.append((w * PARTS + y * SIDE + x, w * PARTS + to_y * SIDE + to_x))
    return pairs


def call(kernel, outs, limit, *operands, scratch=(), scalars=0, far=0, held=0):
    near = len(operands) - far
    specs = [SMEM] * scalars + [VMEM] * (near - scalars) + [HBM] * far
    size = sum(o.size * o.dtype.itemsize for o in operands)
    places = [None] * (near - held) + [pltpu.VMEM] * held + [pltpu.HBM] * far
    operands = [
        o if place is None else pltpu.with_memory_space_constraint(o, place)
        for o, place in zip(operands, places)
    ]
    return pl.pallas_call(
        kernel,
        out_shape=[jax.ShapeDtypeStruct(shape, kind) for shape, kind in outs],
        in_specs=specs,
        out_specs=[VMEM] * len(outs),
        scratch_shapes=scratch,
        compiler_params=pltpu.CompilerParams(vmem_limit_bytes=limit),
        cost_estimate=pl.CostEstimate(flops=0, bytes_accessed=size, transcendentals=0),
    )(*operands)


def reach(squares):
    return REACH * lax.rsqrt(jnp.maximum(squares, 1e-30))


def write_norm(squares):
    rest = squares * lax.rsqrt(jnp.maximum(squares, 1e-30))
    lane = lax.broadcasted_iota(jnp.int32, (squares.shape[0], LANES), 1)
    tile = jnp.zeros((squares.shape[0], LANES), F32)
    for i, factor in enumerate(NORM_SCALES):
        part = rest * factor
        if i < 2:
            part = part.astype(BF16).astype(F32)
            part = jnp.where(jnp.abs(part) < 2.0**-10, 0.0, part)
        rest = rest - part * (1.0 / factor)
        tile = jnp.where(lane == i, part, tile)
    return tile


def read_norm(tile):
    parts = [tile[:, i : i + 1] * (1.0 / factor) for i, factor in enumerate(NORM_SCALES)]
    return (parts[0] + parts[1]) + parts[2]


def weighted(refs):
    last = refs[0].shape[1] - LANES
    norms = [read_norm(ref[:, pl.ds(last, LANES)]) for ref in refs]
    squares = [norm * norm for norm in norms]
    weights = [norm * (1.0 / REACH) for norm in norms]

    def total(at, size):
        parts = [ref[:, pl.ds(at, size)] * weight for ref, weight in zip(refs, weights)]
        return (parts[0] + parts[1]) + (parts[2] + parts[3])

    return total, (squares[0] + squares[1]) + (squares[2] + squares[3])


def project_kernel(
    len_ref, blocks_ref, core_ref, cos_ref, sin_ref, x_hbm, gain_hbm, wq_hbm, wk_hbm, wv_hbm, out_ref, stream_ref, x_ref, gain_ref, wq_ref, wk_ref,
    wv_ref, sems,
):
    pairs = ((x_hbm, x_ref), (gain_hbm, gain_ref), (wq_hbm, wq_ref), (wk_hbm, wk_ref), (wv_hbm, wv_ref))
    copies = [pltpu.make_async_copy(a, b, sems.at[i]) for i, (a, b) in enumerate(pairs)]
    for copy in copies:
        copy.start()
    copies[0].wait()
    copies[1].wait()
    rows = x_ref.shape[1] // PARTS
    for n in range(PARTS):
        for m in range(2):
            stream_ref[pl.ds((n * 2 + m) * rows, rows), :] = x_ref[m, pl.ds(n * rows, rows), :]
    stream = stream_ref[...]
    squares = jnp.sum(stream * stream, axis=-1, keepdims=True)
    scale = reach(squares)
    normed = (stream * gain_ref[...]).astype(BF16)
    at = 0
    for copy, w_ref in zip(copies[2:], (wq_ref, wk_ref, wv_ref)):
        copy.wait()
        width = w_ref.shape[1]
        product = jnp.dot(normed, w_ref[...], preferred_element_type=F32)
        out_ref[:, pl.ds(at, width)] = product * scale
        at += width
    out_ref[:, pl.ds(at, LANES)] = write_norm(squares)


def total_kernel(core_ref, mine_ref, other_ref, total_ref, half_ref):
    total = (mine_ref[...] + other_ref[...]).astype(BF16)
    total_ref[...] = total
    half = half_ref.shape[0]
    half_ref[...] = jnp.where(core_ref[0] == 0, total[:half, :], total[half:, :])


def pack_kernel(near_ref, far_ref, out_ref):
    rows = near_ref.shape[0]
    out_ref[pl.ds(0, rows), :] = near_ref[...]
    out_ref[pl.ds(rows, far_ref.shape[0]), :] = far_ref[...]


def attend_kernel(
    len_ref, total_ref, squares_ref, cos_ref, sin_ref, keys_hbm, values_hbm, out_ref, q_s, a_s, s_s, keys_s, values_s,
    key_sems, value_sems,
):
    here = total_ref.shape[0]
    cache = keys_s.shape[1]
    chunk = 512
    counts = [lax.shift_right_logical(len_ref[r] + (chunk - 1), 9) for r in range(here)]

    def fetch(far, near, sems, r, j):
        part = pl.ds(pl.multiple_of(j * chunk, chunk), chunk)
        return pltpu.make_async_copy(far.at[r, part], near.at[r, part], sems.at[r, j])

    def start(far, near, sems, r):
        @pl.loop(0, counts[r])
        def _(j):
            fetch(far, near, sems, r, j).start()

    def finish(far, near, sems, r):
        @pl.loop(0, counts[r])
        def _(j):
            fetch(far, near, sems, r, j).wait()

    for r in range(here):
        start(keys_hbm, keys_s, key_sems, r)
    for r in range(here):
        start(values_hbm, values_s, value_sems, r)
    for r in range(here):

        @pl.loop(counts[r], cache // chunk)
        def _(j):
            part = pl.ds(pl.multiple_of(j * chunk, chunk), chunk)
            values_s[r, part, :] = jnp.zeros((chunk, HEAD), BF16)

    total = total_ref[...]
    heads = out_ref.shape[2] // HEAD
    split = heads * HEAD
    factor = lax.rsqrt(squares_ref[...] / D + EPSILON)
    cos, sin = cos_ref[...], sin_ref[...]

    def turned(part):
        part = part * factor
        return (part * cos + pltpu.roll(part, HEAD // 2, 1) * sin).astype(BF16).astype(F32)

    key_new = turned(total[:, split : split + HEAD])
    value_new = (total[:, split + HEAD :] * factor).astype(BF16).astype(F32)
    for h in range(heads):
        q_s[:, h, :] = turned(total[:, h * HEAD : (h + 1) * HEAD])
    scaling = HEAD ** (-0.5)
    position = lax.broadcasted_iota(jnp.int32, (1, cache), 1)
    for r in range(here):
        finish(keys_hbm, keys_s, key_sems, r)
    own = []
    for r in range(here):
        queries = q_s[r]
        scores = lax.dot_general(
            queries.astype(BF16),
            keys_s[r],
            (((1,), (1,)), ((), ())),
            preferred_element_type=F32,
        )
        s_s[pl.ds(r * heads, heads), :] = jnp.where(
            position < len_ref[r], scores * scaling, -jnp.inf
        )
        own.append(jnp.sum(queries * key_new[r : r + 1, :], axis=-1, keepdims=True) * scaling)
    weights, own_weights = [], []
    for r in range(here):
        scores = s_s[pl.ds(r * heads, heads), :]
        highest = jnp.maximum(jnp.max(scores, axis=-1, keepdims=True), own[r])
        shifted = jnp.exp(scores - highest)
        own_term = jnp.exp(own[r] - highest)
        totals = jnp.sum(shifted, axis=-1, keepdims=True) + own_term
        weights.append((shifted / totals).astype(BF16))
        own_weights.append((own_term / totals).astype(BF16).astype(F32))
    for r in range(here):
        finish(values_hbm, values_s, value_sems, r)
    for r in range(here):
        attended = jnp.dot(weights[r], values_s[r], preferred_element_type=F32)
        a_s[r] = attended + own_weights[r] * value_new[r : r + 1, :]
    for h in range(heads):
        part = a_s[:, h, :].astype(BF16)
        for n in range(PARTS):
            out_ref[n, :, pl.ds(h * HEAD, HEAD)] = part


def wide_total(refs):
    core_ref, mine_ref, near_ref, far_ref, other_ref = refs
    half = far_ref.shape[0]
    rows = mine_ref.shape[0]
    first = core_ref[0] == 0
    far, far_other = far_ref[...].astype(F32), other_ref[pl.ds(rows, half), :].astype(F32)
    opposite = jnp.concatenate(
        [jnp.where(first, far, far_other), jnp.where(first, far_other, far)], axis=0
    )
    sides = near_ref[...].astype(F32) + other_ref[pl.ds(0, rows), :].astype(F32)
    return (mine_ref[...].astype(F32) + opposite) + sides


def gate_kernel(
    core_ref, blocks_ref, mine_ref, near_ref, far_ref, other_ref, stream_ref, gain_ref, wg_ref,
    wu_ref, middle_ref, out0_ref, out1_ref, out2_ref, out3_ref, sorted_s, normed_s,
):
    middle_ref[...] = stream_ref[...] + wide_total(
        (core_ref, mine_ref, near_ref, far_ref, other_ref)
    )
    rows = middle_ref.shape[0] // PARTS
    for i in range(PARTS):
        start = pl.multiple_of(blocks_ref[i] * rows, rows)
        sorted_s[pl.ds(i * rows, rows), :] = middle_ref[pl.ds(start, rows), :]
    middle = sorted_s[...]
    squares = jnp.sum(middle * middle, axis=-1, keepdims=True)
    scale, norm = reach(squares), write_norm(squares)
    normed_s[...] = (middle * gain_ref[...]).astype(BF16)
    outs = (out0_ref, out1_ref, out2_ref, out3_ref)
    units = wg_ref.shape[1]
    group = middle.shape[0] // SIDE
    tile = 512
    normed = normed_s[...]
    for at, w_ref in ((0, wg_ref), (units, wu_ref)):
        for j in range(0, units, tile):
            product = jnp.dot(normed, w_ref[:, pl.ds(j, tile)], preferred_element_type=F32) * scale
            for d in range(SIDE):
                outs[d][:, pl.ds(at + j, tile)] = product[d * group : (d + 1) * group, :]
    for d in range(SIDE):
        outs[d][:, pl.ds(2 * units, LANES)] = norm[d * group : (d + 1) * group, :]


def middle_sum_kernel(a_ref, b_ref, c_ref, d_ref, out0_ref, out1_ref, out2_ref, out3_ref):
    last = a_ref.shape[1] - LANES
    tile = 1024
    rows = a_ref.shape[0] // SIDE
    total, squares = weighted((a_ref, b_ref, c_ref, d_ref))
    scale = reach(squares)
    outs = (out0_ref, out1_ref, out2_ref, out3_ref)

    def put(at, size, value):
        for k in range(SIDE):
            outs[k][:, pl.ds(at, size)] = value[k * rows : (k + 1) * rows, :]

    for at in range(0, last, tile):
        put(at, tile, total(at, tile) * scale)
    put(last, LANES, write_norm(squares))


def hidden_kernel(a_ref, b_ref, c_ref, d_ref, out_ref):
    units = out_ref.shape[2]
    tile = 512
    total, squares = weighted((a_ref, b_ref, c_ref, d_ref))
    factor = lax.rsqrt(squares / D + EPSILON)
    for at in range(0, units, tile):
        gate = total(at, tile) * factor
        up = total(units + at, tile) * factor
        hidden = (gate / (1.0 + jnp.exp(-gate)) * up).astype(BF16)
        for n in range(PARTS):
            out_ref[n, :, pl.ds(at, tile)] = hidden


def finish_kernel(core_ref, mine_ref, near_ref, far_ref, other_ref, middle_ref, out_ref):
    result = middle_ref[...] + wide_total((core_ref, mine_ref, near_ref, far_ref, other_ref))
    rows = out_ref.shape[1] // PARTS
    for n in range(PARTS):
        for m in range(2):
            at = (n * 2 + m) * rows
            out_ref[m, pl.ds(n * rows, rows), :] = result[at : at + rows, :]


def exchange(payload):
    return lax.all_to_all(payload, "narrow", 0, 0, tiled=True)


def move(sends, stage):
    taken = {}
    for step in (1, 3, 2):
        block = sends[step - 1].astype(F16)
        taken[step] = lax.ppermute(block, ("wide", "narrow"), plane_pairs(step, stage)).astype(F32)
    return [taken[step] for step in (1, 2, 3)]


def sum_wide_parts(partial, core_flag):
    rows, width = partial.shape
    half = rows // 2
    mine, part = call(
        total_kernel,
        [((rows, width), BF16), ((half, width), BF16)],
        4 * MIB,
        core_flag,
        partial,
        lax.ppermute(partial, "wide", CORE_SWAP),
        scalars=1,
    )
    near = lax.ppermute(mine, "wide", NEXT_Z)
    far = lax.ppermute(part, "wide", FAR_Z)
    (both,) = call(pack_kernel, [((rows + half, width), BF16)], 4 * MIB, near, far)
    other = lax.ppermute(both, "wide", CORE_SWAP)
    return mine, near, far, other


def body(
    hidden_in,
    attn_gain,
    w_query,
    w_key,
    w_value,
    w_out,
    ffn_gain,
    w_gate,
    w_up,
    w_down,
    key_cache,
    value_cache,
    cache_len,
):
    micro, _, width = hidden_in.shape
    rows = key_cache.shape[1]
    here = micro * rows
    every = here * PARTS
    split = w_query.shape[1]
    units = w_gate.shape[1]
    core = lax.axis_index("wide") % 2
    at_y, at_x = lax.axis_index("narrow") // SIDE, lax.axis_index("narrow") % SIDE
    first, second = jnp.arange(PARTS) // SIDE, jnp.arange(PARTS) % SIDE
    step_y = jnp.where(core == 0, second, first)
    step_x = jnp.where(core == 0, first, second)
    blocks = ((at_y + step_y) % SIDE * SIDE + (at_x + step_x) % SIDE).astype(jnp.int32)
    core_flag = core.astype(jnp.int32)[None]

    lengths = cache_len.reshape(here)
    half = HEAD // 2
    base = 500000.0 ** (-jnp.arange(half, dtype=F32) * 2.0 / HEAD)
    angles = lengths.astype(F32)[:, None] * base[None]
    cosines, sines = jnp.cos(angles), jnp.sin(angles)
    cosines = jnp.concatenate([cosines, cosines], axis=-1)
    sines = jnp.concatenate([-sines, sines], axis=-1)

    payload, stream = call(
        project_kernel,
        [((every, split + 3 * HEAD), F32), ((every, width), F32)],
        8 * MIB,
        lengths,
        blocks,
        core_flag,
        cosines,
        sines,
        hidden_in,
        attn_gain[None],
        w_query,
        w_key,
        w_value,
        scalars=3,
        far=5,
        scratch=[pltpu.VMEM(hidden_in.shape, F32), pltpu.VMEM((1, width), F32)]
        + [pltpu.VMEM(w.shape, BF16) for w in (w_query, w_key, w_value)]
        + [pltpu.SemaphoreType.DMA((5,))],
    )
    got = exchange(payload.astype(F16).reshape(PARTS, here, -1)).astype(F32)
    norms = got[:, :, split + 2 * HEAD :][:, :, : len(NORM_SCALES)]
    norms = jnp.sum(norms * (1.0 / jnp.array(NORM_SCALES, F32)), axis=-1, keepdims=True)
    total = jnp.sum(got[:, :, : split + 2 * HEAD] * (norms * (1.0 / REACH)), axis=0)
    squares = jnp.sum(norms * norms, axis=0)

    (attended,) = call(
        attend_kernel,
        [((PARTS, here, split), BF16)],
        16 * MIB,
        lengths,
        total,
        squares,
        cosines,
        sines,
        key_cache.reshape(here, -1, HEAD),
        value_cache.reshape(here, -1, HEAD),
        scalars=1,
        far=2,
        scratch=[pltpu.VMEM((here, split // HEAD, HEAD), F32)] * 2
        + [pltpu.VMEM((here * split // HEAD, key_cache.shape[3]), F32)]
        + [pltpu.VMEM((here, key_cache.shape[3], HEAD), BF16)] * 2
        + [pltpu.SemaphoreType.DMA((here, key_cache.shape[3] // 512))] * 2,
    )
    gathered = exchange(attended).reshape(every, split)
    parts = sum_wide_parts(jnp.dot(gathered, w_out, preferred_element_type=F32), core_flag)
    group = every // SIDE
    full = 2 * units + LANES
    middle, own, *sends = call(
        gate_kernel,
        [((every, width), F32)] + [((group, full), F32)] * SIDE,
        8 * MIB,
        core_flag,
        blocks,
        *parts,
        stream,
        ffn_gain[None],
        w_gate,
        w_up,
        scalars=2,
        held=2,
        scratch=[pltpu.VMEM((every, width), F32), pltpu.VMEM((every, width), BF16)],
    )
    taken = move(sends, 0)
    own, *sends = call(middle_sum_kernel, [((here, full), F32)] * SIDE, 8 * MIB, own, *taken)
    taken = move(sends, 1)
    (hidden,) = call(hidden_kernel, [((PARTS, here, units), BF16)], 8 * MIB, own, *taken)
    gathered = exchange(hidden).reshape(every, units)
    parts = sum_wide_parts(jnp.dot(gathered, w_down, preferred_element_type=F32), core_flag)
    (result,) = call(
        finish_kernel, [(hidden_in.shape, F32)], 8 * MIB, core_flag, *parts, middle, scalars=1
    )
    return result


def solution(mesh):
    return jax.shard_map(
        body,
        mesh=mesh,
        in_specs=(
            P(None, None, "narrow"),
            P("narrow"),
            P("narrow", "wide"),
            P("narrow", "wide"),
            P("narrow", "wide"),
            P("wide", "narrow"),
            P("narrow"),
            P("narrow", "wide"),
            P("narrow", "wide"),
            P("wide", "narrow"),
            P(None, "narrow", "wide", None, None),
            P(None, "narrow", "wide", None, None),
            P(None, "narrow"),
        ),
        out_specs=P(None, None, "narrow"),
        check_vma=False,
    )
```

```python
import functools

import jax
import jax.numpy as jnp
from jax import lax
from jax.experimental import pallas as pl
from jax.experimental.pallas import tpu as pltpu
from jax.sharding import PartitionSpec as P

D = 8192
EPSILON = 1e-05
BF16 = jnp.bfloat16
F16 = jnp.float16
F32 = jnp.float32
SIDE = 4
PARTS = SIDE * SIDE
HEAD = 128
LANES = 128
VMEM = pl.BlockSpec(memory_space=pltpu.VMEM)
HBM = pl.BlockSpec(memory_space=pltpu.HBM)
SMEM = pl.BlockSpec(memory_space=pltpu.SMEM)
KIB = 1 << 10
MIB = 1 << 20
REACH = 8192.0
NORM_SCALES = (2.0**-2, 2.0**6, 2.0**16)


def wide_pairs(target):
    pairs = []
    for z in range(SIDE):
        for c in range(2):
            to_z, to_c = target(z, c)
            pairs.append((z * 2 + c, to_z % SIDE * 2 + to_c))
    return pairs


CORE_SWAP = wide_pairs(lambda z, c: (z, 1 - c))
NEXT_Z = wide_pairs(lambda z, c: (z + 1 if c == 0 else z - 1, c))
FAR_Z = wide_pairs(lambda z, c: (z + 2, c))


def plane_pairs(step, stage):
    pairs = []
    for w in range(2 * SIDE):
        for y in range(SIDE):
            for x in range(SIDE):
                along_x = (w % 2 == 0) == (stage == 0)
                to_y, to_x = (y, (x + step) % SIDE) if along_x else ((y + step) % SIDE, x)
                pairs.append((w * PARTS + y * SIDE + x, w * PARTS + to_y * SIDE + to_x))
    return pairs


def call(kernel, outs, limit, *operands, scratch=(), scalars=0, far=0, held=0, kept=0):
    near = len(operands) - far
    specs = [SMEM] * scalars + [VMEM] * (near - scalars) + [HBM] * far
    size = sum(o.size * o.dtype.itemsize for o in operands)
    places = [None] * (near - held) + [pltpu.VMEM] * held + [pltpu.HBM] * far
    operands = [
        o if place is None else pltpu.with_memory_space_constraint(o, place)
        for o, place in zip(operands, places)
    ]
    return pl.pallas_call(
        kernel,
        out_shape=[
            (jax.ShapeDtypeStruct if i < len(outs) - kept else pltpu.VMEM)(shape, kind)
            for i, (shape, kind) in enumerate(outs)
        ],
        in_specs=specs,
        out_specs=[VMEM] * len(outs),
        scratch_shapes=scratch,
        compiler_params=pltpu.CompilerParams(vmem_limit_bytes=limit),
        cost_estimate=pl.CostEstimate(flops=0, bytes_accessed=size, transcendentals=0),
    )(*operands)


def reach(squares):
    return REACH * lax.rsqrt(jnp.maximum(squares, 1e-30))


def write_norm(squares):
    rest = squares * lax.rsqrt(jnp.maximum(squares, 1e-30))
    lane = lax.broadcasted_iota(jnp.int32, (squares.shape[0], LANES), 1)
    tile = jnp.zeros((squares.shape[0], LANES), F32)
    for i, factor in enumerate(NORM_SCALES):
        part = rest * factor
        if i < 2:
            part = part.astype(BF16).astype(F32)
            part = jnp.where(jnp.abs(part) < 2.0**-10, 0.0, part)
        rest = rest - part * (1.0 / factor)
        tile = jnp.where(lane == i, part, tile)
    return tile


def read_norm(tile):
    parts = [tile[:, i : i + 1] * (1.0 / factor) for i, factor in enumerate(NORM_SCALES)]
    return (parts[0] + parts[1]) + parts[2]


def weighted(refs):
    last = refs[0].shape[1] - LANES
    norms = [read_norm(ref[:, pl.ds(last, LANES)]) for ref in refs]
    squares = [norm * norm for norm in norms]
    weights = [norm * (1.0 / REACH) for norm in norms]

    def total(at, size):
        parts = [ref[:, pl.ds(at, size)] * weight for ref, weight in zip(refs, weights)]
        return (parts[0] + parts[1]) + (parts[2] + parts[3])

    return total, (squares[0] + squares[1]) + (squares[2] + squares[3])


def project_kernel(
    len_ref, blocks_ref, core_ref, cos_ref, sin_ref, x_hbm, gain_hbm, wq_hbm, wk_hbm, wv_hbm,
    keys_hbm, values_hbm, out_ref, stream_ref, keys_s, values_s, x_ref, gain_ref, wq_ref, wk_ref,
    wv_ref, sems, key_sems, value_sems,
):
    pairs = ((x_hbm, x_ref), (gain_hbm, gain_ref), (wq_hbm, wq_ref), (wk_hbm, wk_ref), (wv_hbm, wv_ref))
    copies = [pltpu.make_async_copy(a, b, sems.at[i]) for i, (a, b) in enumerate(pairs)]
    for copy in copies:
        copy.start()
    chunk = 512
    here, cache = keys_s.shape[0], keys_s.shape[1]
    counts = [lax.shift_right_logical(len_ref[r] + (chunk - 1), 9) for r in range(here)]

    def fetch(far, near, sems, r, j):
        part = pl.ds(pl.multiple_of(j * chunk, chunk), chunk)
        return pltpu.make_async_copy(far.at[r, part], near.at[r, part], sems.at[r, j])

    def start(far, near, sems, r):
        @pl.loop(0, counts[r])
        def _(j):
            fetch(far, near, sems, r, j).start()

    def finish(far, near, sems, r):
        @pl.loop(0, counts[r])
        def _(j):
            fetch(far, near, sems, r, j).wait()

    for r in range(here):
        start(keys_hbm, keys_s, key_sems, r)
    for r in range(here):
        start(values_hbm, values_s, value_sems, r)
    for r in range(here):

        @pl.loop(counts[r], cache // chunk)
        def _(j):
            part = pl.ds(pl.multiple_of(j * chunk, chunk), chunk)
            values_s[r, part, :] = jnp.zeros((chunk, HEAD), BF16)
    copies[0].wait()
    copies[1].wait()
    rows = x_ref.shape[1] // PARTS
    for n in range(PARTS):
        for m in range(2):
            stream_ref[pl.ds((n * 2 + m) * rows, rows), :] = x_ref[m, pl.ds(n * rows, rows), :]
    stream = stream_ref[...]
    squares = jnp.sum(stream * stream, axis=-1, keepdims=True)
    scale = reach(squares)
    normed = (stream * gain_ref[...]).astype(BF16)
    at = 0
    for copy, w_ref in zip(copies[2:], (wq_ref, wk_ref, wv_ref)):
        copy.wait()
        width = w_ref.shape[1]
        product = jnp.dot(normed, w_ref[...], preferred_element_type=F32)
        out_ref[:, pl.ds(at, width)] = product * scale
        at += width
    out_ref[:, pl.ds(at, LANES)] = write_norm(squares)
    for r in range(here):
        finish(keys_hbm, keys_s, key_sems, r)
        finish(values_hbm, values_s, value_sems, r)


def total_kernel(core_ref, mine_ref, other_ref, total_ref, half_ref):
    total = (mine_ref[...] + other_ref[...]).astype(BF16)
    total_ref[...] = total
    half = half_ref.shape[0]
    half_ref[...] = jnp.where(core_ref[0] == 0, total[:half, :], total[half:, :])


def attend_kernel(
    len_ref, total_ref, squares_ref, cos_ref, sin_ref, keys_ref, values_ref, out_ref, q_s, a_s, s_s,
):
    here = total_ref.shape[0]
    cache = keys_ref.shape[1]
    total = total_ref[...]
    heads = out_ref.shape[2] // HEAD
    split = heads * HEAD
    factor = lax.rsqrt(squares_ref[:, 0:1] / D + EPSILON)
    cos, sin = cos_ref[...], sin_ref[...]

    def turned(part):
        part = part * factor
        return (part * cos + pltpu.roll(part, HEAD // 2, 1) * sin).astype(BF16).astype(F32)

    key_new = turned(total[:, split : split + HEAD])
    value_new = (total[:, split + HEAD :] * factor).astype(BF16).astype(F32)
    for h in range(heads):
        q_s[:, h, :] = turned(total[:, h * HEAD : (h + 1) * HEAD])
    scaling = HEAD ** (-0.5)
    position = lax.broadcasted_iota(jnp.int32, (1, cache), 1)
    own = []
    for r in range(here):
        queries = q_s[r]
        scores = lax.dot_general(
            queries.astype(BF16),
            keys_ref[r],
            (((1,), (1,)), ((), ())),
            preferred_element_type=F32,
        )
        s_s[pl.ds(r * heads, heads), :] = jnp.where(
            position < len_ref[r], scores * scaling, -jnp.inf
        )
        own.append(jnp.sum(queries * key_new[r : r + 1, :], axis=-1, keepdims=True) * scaling)
    weights, own_weights = [], []
    for r in range(here):
        scores = s_s[pl.ds(r * heads, heads), :]
        highest = jnp.maximum(jnp.max(scores, axis=-1, keepdims=True), own[r])
        shifted = jnp.exp(scores - highest)
        own_term = jnp.exp(own[r] - highest)
        totals = jnp.sum(shifted, axis=-1, keepdims=True) + own_term
        weights.append((shifted / totals).astype(BF16))
        own_weights.append((own_term / totals).astype(BF16).astype(F32))
    for r in range(here):
        attended = jnp.dot(weights[r], values_ref[r], preferred_element_type=F32)
        a_s[r] = attended + own_weights[r] * value_new[r : r + 1, :]
    for h in range(heads):
        part = a_s[:, h, :].astype(BF16)
        for n in range(PARTS):
            out_ref[n, :, pl.ds(h * HEAD, HEAD)] = part


def wide_total(refs):
    core_ref, mine_ref, near_ref, other_near_ref, far_ref, other_far_ref = refs
    first = core_ref[0] == 0
    far, far_other = far_ref[...].astype(F32), other_far_ref[...].astype(F32)
    opposite = jnp.concatenate(
        [jnp.where(first, far, far_other), jnp.where(first, far_other, far)], axis=0
    )
    sides = near_ref[...].astype(F32) + other_near_ref[...].astype(F32)
    return (mine_ref[...].astype(F32) + opposite) + sides


def gate_kernel(
    core_ref, blocks_ref, mine_ref, near_ref, other_near_ref, far_ref, other_far_ref, stream_ref, gain_ref,
    wg_ref, wu_ref, middle_ref, out0_ref, out1_ref, out2_ref, out3_ref, sorted_s, normed_s,
):
    middle_ref[...] = stream_ref[...] + wide_total(
        (core_ref, mine_ref, near_ref, other_near_ref, far_ref, other_far_ref)
    )
    rows = middle_ref.shape[0] // PARTS
    for i in range(PARTS):
        start = pl.multiple_of(blocks_ref[i] * rows, rows)
        sorted_s[pl.ds(i * rows, rows), :] = middle_ref[pl.ds(start, rows), :]
    middle = sorted_s[...]
    squares = jnp.sum(middle * middle, axis=-1, keepdims=True)
    scale, norm = reach(squares), write_norm(squares)
    normed_s[...] = (middle * gain_ref[...]).astype(BF16)
    outs = (out0_ref, out1_ref, out2_ref, out3_ref)
    units = wg_ref.shape[1]
    group = middle.shape[0] // SIDE
    tile = 512
    normed = normed_s[...]
    for at, w_ref in ((0, wg_ref), (units, wu_ref)):
        for j in range(0, units, tile):
            product = jnp.dot(normed, w_ref[:, pl.ds(j, tile)], preferred_element_type=F32) * scale
            for d in range(SIDE):
                outs[d][:, pl.ds(at + j, tile)] = product[d * group : (d + 1) * group, :]
    for d in range(SIDE):
        outs[d][:, pl.ds(2 * units, LANES)] = norm[d * group : (d + 1) * group, :]


def middle_sum_kernel(a_ref, b_ref, c_ref, d_ref, out0_ref, out1_ref, out2_ref, out3_ref):
    last = a_ref.shape[1] - LANES
    tile = 1024
    rows = a_ref.shape[0] // SIDE
    total, squares = weighted((a_ref, b_ref, c_ref, d_ref))
    scale = reach(squares)
    outs = (out0_ref, out1_ref, out2_ref, out3_ref)

    def put(at, size, value):
        for k in range(SIDE):
            outs[k][:, pl.ds(at, size)] = value[k * rows : (k + 1) * rows, :]

    for at in range(0, last, tile):
        put(at, tile, total(at, tile) * scale)
    put(last, LANES, write_norm(squares))


def hidden_kernel(a_ref, b_ref, c_ref, d_ref, out_ref):
    units = out_ref.shape[2]
    tile = 512
    total, squares = weighted((a_ref, b_ref, c_ref, d_ref))
    factor = lax.rsqrt(squares / D + EPSILON)
    for at in range(0, units, tile):
        gate = total(at, tile) * factor
        up = total(units + at, tile) * factor
        hidden = (gate / (1.0 + jnp.exp(-gate)) * up).astype(BF16)
        for n in range(PARTS):
            out_ref[n, :, pl.ds(at, tile)] = hidden


def finish_kernel(
    core_ref, mine_ref, near_ref, other_near_ref, far_ref, other_far_ref, middle_ref, out_ref
):
    result = middle_ref[...] + wide_total((core_ref, mine_ref, near_ref, other_near_ref, far_ref, other_far_ref))
    rows = out_ref.shape[1] // PARTS
    for n in range(PARTS):
        for m in range(2):
            at = (n * 2 + m) * rows
            out_ref[m, pl.ds(n * rows, rows), :] = result[at : at + rows, :]


def exchange(payload):
    return lax.all_to_all(payload, "narrow", 0, 0, tiled=True)


def move(sends, stage):
    taken = {}
    for step in (1, 3, 2):
        block = sends[step - 1].astype(F16)
        taken[step] = lax.ppermute(block, ("wide", "narrow"), plane_pairs(step, stage)).astype(F32)
    return [taken[step] for step in (1, 2, 3)]


def sum_wide_parts(partial, core_flag):
    rows, width = partial.shape
    half = rows // 2
    mine, part = call(
        total_kernel,
        [((rows, width), BF16), ((half, width), BF16)],
        4 * MIB,
        core_flag,
        partial,
        lax.ppermute(partial, "wide", CORE_SWAP),
        scalars=1,
    )
    near = lax.ppermute(mine, "wide", NEXT_Z)
    far = lax.ppermute(part, "wide", FAR_Z)
    other_near = lax.ppermute(near, "wide", CORE_SWAP)
    other_far = lax.ppermute(far, "wide", CORE_SWAP)
    return mine, near, other_near, far, other_far


def body(
    hidden_in,
    attn_gain,
    w_query,
    w_key,
    w_value,
    w_out,
    ffn_gain,
    w_gate,
    w_up,
    w_down,
    key_cache,
    value_cache,
    cache_len,
):
    micro, _, width = hidden_in.shape
    rows = key_cache.shape[1]
    here = micro * rows
    every = here * PARTS
    split = w_query.shape[1]
    units = w_gate.shape[1]
    core = lax.axis_index("wide") % 2
    at_y, at_x = lax.axis_index("narrow") // SIDE, lax.axis_index("narrow") % SIDE
    first, second = jnp.arange(PARTS) // SIDE, jnp.arange(PARTS) % SIDE
    step_y = jnp.where(core == 0, second, first)
    step_x = jnp.where(core == 0, first, second)
    blocks = ((at_y + step_y) % SIDE * SIDE + (at_x + step_x) % SIDE).astype(jnp.int32)
    core_flag = core.astype(jnp.int32)[None]

    lengths = cache_len.reshape(here)
    half = HEAD // 2
    base = 500000.0 ** (-jnp.arange(half, dtype=F32) * 2.0 / HEAD)
    angles = lengths.astype(F32)[:, None] * base[None]
    cosines, sines = jnp.cos(angles), jnp.sin(angles)
    cosines = jnp.concatenate([cosines, cosines], axis=-1)
    sines = jnp.concatenate([-sines, sines], axis=-1)

    held = (here, key_cache.shape[3], HEAD)
    payload, stream, keys, values = call(
        project_kernel,
        [((every, split + 3 * HEAD), F32), ((every, width), F32)] + [(held, BF16)] * 2,
        8 * MIB,
        lengths,
        blocks,
        core_flag,
        cosines,
        sines,
        hidden_in,
        attn_gain[None],
        w_query,
        w_key,
        w_value,
        key_cache.reshape(held),
        value_cache.reshape(held),
        scalars=3,
        far=7,
        kept=2,
        scratch=[pltpu.VMEM(hidden_in.shape, F32), pltpu.VMEM((1, width), F32)]
        + [pltpu.VMEM(w.shape, BF16) for w in (w_query, w_key, w_value)]
        + [pltpu.SemaphoreType.DMA((5,))]
        + [pltpu.SemaphoreType.DMA((here, held[1] // 512))] * 2,
    )
    got = exchange(payload.astype(F16).reshape(PARTS, here, -1))
    last = split + 2 * HEAD
    norms = got[:, :, last : last + len(NORM_SCALES)].astype(F32)
    norms = jnp.sum(norms * (1.0 / jnp.array(NORM_SCALES, F32)), axis=-1, keepdims=True)
    total = jnp.sum(got[:, :, :last].astype(F32) * (norms * (1.0 / REACH)), axis=0)
    squares = jnp.sum(jnp.broadcast_to(norms * norms, (PARTS, here, LANES)), axis=0)

    (attended,) = call(
        attend_kernel,
        [((PARTS, here, split), BF16)],
        16 * MIB,
        lengths,
        total,
        squares,
        cosines,
        sines,
        keys,
        values,
        scalars=1,
        held=2,
        scratch=[pltpu.VMEM((here, split // HEAD, HEAD), F32)] * 2
        + [pltpu.VMEM((here * split // HEAD, held[1]), F32)],
    )
    gathered = exchange(attended).reshape(every, split)
    parts = sum_wide_parts(jnp.dot(gathered, w_out, preferred_element_type=F32), core_flag)
    group = every // SIDE
    full = 2 * units + LANES
    middle, own, *sends = call(
        gate_kernel,
        [((every, width), F32)] + [((group, full), F32)] * SIDE,
        8 * MIB,
        core_flag,
        blocks,
        *parts,
        stream,
        ffn_gain[None],
        w_gate,
        w_up,
        scalars=2,
        held=2,
        scratch=[pltpu.VMEM((every, width), F32), pltpu.VMEM((every, width), BF16)],
    )
    taken = move(sends, 0)
    own, *sends = call(middle_sum_kernel, [((here, full), F32)] * SIDE, 8 * MIB, own, *taken)
    taken = move(sends, 1)
    (hidden,) = call(hidden_kernel, [((PARTS, here, units), BF16)], 8 * MIB, own, *taken)
    gathered = exchange(hidden).reshape(every, units)
    parts = sum_wide_parts(jnp.dot(gathered, w_down, preferred_element_type=F32), core_flag)
    (result,) = call(
        finish_kernel, [(hidden_in.shape, F32)], 8 * MIB, core_flag, *parts, middle, scalars=1
    )
    return result


def solution(mesh):
    return jax.shard_map(
        body,
        mesh=mesh,
        in_specs=(
            P(None, None, "narrow"),
            P("narrow"),
            P("narrow", "wide"),
            P("narrow", "wide"),
            P("narrow", "wide"),
            P("wide", "narrow"),
            P("narrow"),
            P("narrow", "wide"),
            P("narrow", "wide"),
            P("wide", "narrow"),
            P(None, "narrow", "wide", None, None),
            P(None, "narrow", "wide", None, None),
            P(None, "narrow"),
        ),
        out_specs=P(None, None, "narrow"),
        check_vma=False,
    )
```

```python
import functools

import jax
import jax.numpy as jnp
import numpy as np
from jax import lax
from jax.experimental import pallas as pl
from jax.experimental.pallas import tpu as pltpu
from jax.sharding import PartitionSpec as P

D = 8192
EPSILON = 1e-05
BF16 = jnp.bfloat16
F16 = jnp.float16
F32 = jnp.float32
SIDE = 4
PARTS = SIDE * SIDE
HEAD = 128
LANES = 128
VMEM = pl.BlockSpec(memory_space=pltpu.VMEM)
HBM = pl.BlockSpec(memory_space=pltpu.HBM)
SMEM = pl.BlockSpec(memory_space=pltpu.SMEM)
KIB = 1 << 10
MIB = 1 << 20
REACH = 8192.0
NORM_SCALES = (2.0**-2, 2.0**6, 2.0**16)


def wide_pairs(target):
    pairs = []
    for z in range(SIDE):
        for c in range(2):
            to_z, to_c = target(z, c)
            pairs.append((z * 2 + c, to_z % SIDE * 2 + to_c))
    return pairs


CORE_SWAP = wide_pairs(lambda z, c: (z, 1 - c))
NEXT_Z = wide_pairs(lambda z, c: (z + 1 if c == 0 else z - 1, c))
FAR_Z = wide_pairs(lambda z, c: (z + 2, c))


def plane_pairs(step, stage):
    pairs = []
    for w in range(2 * SIDE):
        for y in range(SIDE):
            for x in range(SIDE):
                along_x = (w % 2 == 0) == (stage == 0)
                to_y, to_x = (y, (x + step) % SIDE) if along_x else ((y + step) % SIDE, x)
                pairs.append((w * PARTS + y * SIDE + x, w * PARTS + to_y * SIDE + to_x))
    return pairs


def call(kernel, outs, limit, *operands, scratch=(), scalars=0, far=0, held=0, kept=0):
    near = len(operands) - far
    specs = [SMEM] * scalars + [VMEM] * (near - scalars) + [HBM] * far
    size = sum(o.size * o.dtype.itemsize for o in operands)
    places = [None] * (near - held) + [pltpu.VMEM] * held + [pltpu.HBM] * far
    operands = [
        o if place is None else pltpu.with_memory_space_constraint(o, place)
        for o, place in zip(operands, places)
    ]
    return pl.pallas_call(
        kernel,
        out_shape=[
            (jax.ShapeDtypeStruct if i < len(outs) - kept else pltpu.VMEM)(shape, kind)
            for i, (shape, kind) in enumerate(outs)
        ],
        in_specs=specs,
        out_specs=[VMEM] * len(outs),
        scratch_shapes=scratch,
        compiler_params=pltpu.CompilerParams(vmem_limit_bytes=limit),
        cost_estimate=pl.CostEstimate(flops=0, bytes_accessed=size, transcendentals=0),
    )(*operands)


def reach(squares):
    return REACH * lax.rsqrt(jnp.maximum(squares, 1e-30))


def write_norm(squares):
    rest = squares * lax.rsqrt(jnp.maximum(squares, 1e-30))
    lane = lax.broadcasted_iota(jnp.int32, (squares.shape[0], LANES), 1)
    tile = jnp.zeros((squares.shape[0], LANES), F32)
    for i, factor in enumerate(NORM_SCALES):
        part = rest * factor
        if i < 2:
            part = part.astype(BF16).astype(F32)
            part = jnp.where(jnp.abs(part) < 2.0**-10, 0.0, part)
        rest = rest - part * (1.0 / factor)
        tile = jnp.where(lane == i, part, tile)
    return tile


def read_norm(tile):
    parts = [tile[:, i : i + 1] * (1.0 / factor) for i, factor in enumerate(NORM_SCALES)]
    return (parts[0] + parts[1]) + parts[2]


def weighted(refs):
    last = refs[0].shape[1] - LANES
    norms = [read_norm(ref[:, pl.ds(last, LANES)]) for ref in refs]
    squares = [norm * norm for norm in norms]
    weights = [norm * (1.0 / REACH) for norm in norms]

    def total(at, size):
        parts = [ref[:, pl.ds(at, size)] * weight for ref, weight in zip(refs, weights)]
        return (parts[0] + parts[1]) + (parts[2] + parts[3])

    return total, (squares[0] + squares[1]) + (squares[2] + squares[3])


def project_kernel(
    blocks_ref, core_ref, len_hbm, base_hbm, x_hbm, gain_hbm, wq_hbm, wk_hbm, wv_hbm, keys_hbm, values_hbm,
    out_ref, stream_ref, cos_ref, sin_ref, lengths_ref, keys_s, values_s, len_s, base_ref, x_ref, gain_ref,
    wq_ref, wk_ref, wv_ref, sems, key_sems, value_sems,
):
    pairs = ((x_hbm, x_ref), (gain_hbm, gain_ref), (wq_hbm, wq_ref), (wk_hbm, wk_ref), (wv_hbm, wv_ref))
    copies = [pltpu.make_async_copy(a, b, sems.at[i]) for i, (a, b) in enumerate(pairs)]
    first = pltpu.make_async_copy(len_hbm, len_s, sems.at[5])
    table = pltpu.make_async_copy(base_hbm, base_ref, sems.at[6])
    for copy in (first, *copies, table):
        copy.start()
    first.wait()
    local = len_s.shape[1]
    len_ref = [len_s[r // local, r % local] for r in range(keys_s.shape[0])]
    chunk = 512
    here, cache = keys_s.shape[0], keys_s.shape[1]
    counts = [lax.shift_right_logical(len_ref[r] + (chunk - 1), 9) for r in range(here)]

    def fetch(far, near, sems, r, j):
        part = pl.ds(pl.multiple_of(j * chunk, chunk), chunk)
        return pltpu.make_async_copy(far.at[r, part], near.at[r, part], sems.at[r, j])

    def start(far, near, sems, r):
        @pl.loop(0, counts[r])
        def _(j):
            fetch(far, near, sems, r, j).start()

    def finish(far, near, sems, r):
        @pl.loop(0, counts[r])
        def _(j):
            fetch(far, near, sems, r, j).wait()

    for r in range(here):
        start(keys_hbm, keys_s, key_sems, r)
    for r in range(here):
        start(values_hbm, values_s, value_sems, r)
    for r in range(here):

        @pl.loop(counts[r], cache // chunk)
        def _(j):
            part = pl.ds(pl.multiple_of(j * chunk, chunk), chunk)
            values_s[r, part, :] = jnp.zeros((chunk, HEAD), BF16)
    row = lax.broadcasted_iota(jnp.int32, lengths_ref.shape, 0)
    lengths = jnp.zeros(lengths_ref.shape, jnp.int32)
    for r in range(here):
        lengths = jnp.where(row == r, len_ref[r], lengths)
    lengths_ref[...] = lengths
    table.wait()
    angles = lengths.astype(F32) * base_ref[...]
    lane = lax.broadcasted_iota(jnp.int32, lengths_ref.shape, 1)
    cos_ref[...] = jnp.cos(angles)
    sines = jnp.sin(angles)
    sin_ref[...] = jnp.where(lane < HEAD // 2, -sines, sines)
    copies[0].wait()
    copies[1].wait()
    rows = x_ref.shape[1] // PARTS
    for n in range(PARTS):
        for m in range(2):
            stream_ref[pl.ds((n * 2 + m) * rows, rows), :] = x_ref[m, pl.ds(n * rows, rows), :]
    stream = stream_ref[...]
    squares = jnp.sum(stream * stream, axis=-1, keepdims=True)
    scale = reach(squares)
    normed = (stream * gain_ref[...]).astype(BF16)
    at = 0
    for copy, w_ref in zip(copies[2:], (wq_ref, wk_ref, wv_ref)):
        copy.wait()
        width = w_ref.shape[1]
        product = jnp.dot(normed, w_ref[...], preferred_element_type=F32)
        out_ref[:, pl.ds(at, width)] = product * scale
        at += width
    out_ref[:, pl.ds(at, LANES)] = write_norm(squares)
    for r in range(here):
        finish(keys_hbm, keys_s, key_sems, r)
        finish(values_hbm, values_s, value_sems, r)


def total_kernel(core_ref, mine_ref, other_ref, total_ref, half_ref):
    total = (mine_ref[...] + other_ref[...]).astype(BF16)
    total_ref[...] = total
    half = half_ref.shape[0]
    half_ref[...] = jnp.where(core_ref[0] == 0, total[:half, :], total[half:, :])


def attend_kernel(
    lengths_ref, total_ref, squares_ref, cos_ref, sin_ref, keys_ref, values_ref, out_ref, q_s, a_s, s_s,
):
    here = total_ref.shape[0]
    cache = keys_ref.shape[1]
    total = total_ref[...]
    heads = out_ref.shape[2] // HEAD
    split = heads * HEAD
    factor = lax.rsqrt(squares_ref[:, 0:1] / D + EPSILON)
    cos, sin = cos_ref[...], sin_ref[...]

    def turned(part):
        part = part * factor
        return (part * cos + pltpu.roll(part, HEAD // 2, 1) * sin).astype(BF16).astype(F32)

    key_new = turned(total[:, split : split + HEAD])
    value_new = (total[:, split + HEAD :] * factor).astype(BF16).astype(F32)
    for h in range(heads):
        q_s[:, h, :] = turned(total[:, h * HEAD : (h + 1) * HEAD])
    scaling = HEAD ** (-0.5)
    position = lax.broadcasted_iota(jnp.int32, (1, cache), 1)
    own = []
    for r in range(here):
        queries = q_s[r]
        scores = lax.dot_general(
            queries.astype(BF16),
            keys_ref[r],
            (((1,), (1,)), ((), ())),
            preferred_element_type=F32,
        )
        s_s[pl.ds(r * heads, heads), :] = jnp.where(
            position < lengths_ref[pl.ds(r, 1), pl.ds(0, 1)], scores * scaling, -jnp.inf
        )
        own.append(jnp.sum(queries * key_new[r : r + 1, :], axis=-1, keepdims=True) * scaling)
    weights, own_weights = [], []
    for r in range(here):
        scores = s_s[pl.ds(r * heads, heads), :]
        highest = jnp.maximum(jnp.max(scores, axis=-1, keepdims=True), own[r])
        shifted = jnp.exp(scores - highest)
        own_term = jnp.exp(own[r] - highest)
        totals = jnp.sum(shifted, axis=-1, keepdims=True) + own_term
        weights.append((shifted / totals).astype(BF16))
        own_weights.append((own_term / totals).astype(BF16).astype(F32))
    for r in range(here):
        attended = jnp.dot(weights[r], values_ref[r], preferred_element_type=F32)
        a_s[r] = attended + own_weights[r] * value_new[r : r + 1, :]
    for h in range(heads):
        part = a_s[:, h, :].astype(BF16)
        for n in range(PARTS):
            out_ref[n, :, pl.ds(h * HEAD, HEAD)] = part


def wide_total(refs):
    core_ref, mine_ref, near_ref, other_near_ref, far_ref, other_far_ref = refs
    first = core_ref[0] == 0
    far, far_other = far_ref[...].astype(F32), other_far_ref[...].astype(F32)
    opposite = jnp.concatenate(
        [jnp.where(first, far, far_other), jnp.where(first, far_other, far)], axis=0
    )
    sides = near_ref[...].astype(F32) + other_near_ref[...].astype(F32)
    return (mine_ref[...].astype(F32) + opposite) + sides


def gate_kernel(
    core_ref, blocks_ref, mine_ref, near_ref, other_near_ref, far_ref, other_far_ref, stream_ref, gain_ref,
    wg_ref, wu_ref, middle_ref, out0_ref, out1_ref, out2_ref, out3_ref, sorted_s, normed_s,
):
    middle_ref[...] = stream_ref[...] + wide_total(
        (core_ref, mine_ref, near_ref, other_near_ref, far_ref, other_far_ref)
    )
    rows = middle_ref.shape[0] // PARTS
    for i in range(PARTS):
        start = pl.multiple_of(blocks_ref[i] * rows, rows)
        sorted_s[pl.ds(i * rows, rows), :] = middle_ref[pl.ds(start, rows), :]
    middle = sorted_s[...]
    squares = jnp.sum(middle * middle, axis=-1, keepdims=True)
    scale, norm = reach(squares), write_norm(squares)
    normed_s[...] = (middle * gain_ref[...]).astype(BF16)
    outs = (out0_ref, out1_ref, out2_ref, out3_ref)
    units = wg_ref.shape[1]
    group = middle.shape[0] // SIDE
    tile = 512
    normed = normed_s[...]
    for at, w_ref in ((0, wg_ref), (units, wu_ref)):
        for j in range(0, units, tile):
            product = jnp.dot(normed, w_ref[:, pl.ds(j, tile)], preferred_element_type=F32) * scale
            for d in range(SIDE):
                outs[d][:, pl.ds(at + j, tile)] = product[d * group : (d + 1) * group, :]
    for d in range(SIDE):
        outs[d][:, pl.ds(2 * units, LANES)] = norm[d * group : (d + 1) * group, :]


def middle_sum_kernel(a_ref, b_ref, c_ref, d_ref, out0_ref, out1_ref, out2_ref, out3_ref):
    last = a_ref.shape[1] - LANES
    tile = 1024
    rows = a_ref.shape[0] // SIDE
    total, squares = weighted((a_ref, b_ref, c_ref, d_ref))
    scale = reach(squares)
    outs = (out0_ref, out1_ref, out2_ref, out3_ref)

    def put(at, size, value):
        for k in range(SIDE):
            outs[k][:, pl.ds(at, size)] = value[k * rows : (k + 1) * rows, :]

    for at in range(0, last, tile):
        put(at, tile, total(at, tile) * scale)
    put(last, LANES, write_norm(squares))


def hidden_kernel(a_ref, b_ref, c_ref, d_ref, out_ref):
    units = out_ref.shape[2]
    tile = 512
    total, squares = weighted((a_ref, b_ref, c_ref, d_ref))
    factor = lax.rsqrt(squares / D + EPSILON)
    for at in range(0, units, tile):
        gate = total(at, tile) * factor
        up = total(units + at, tile) * factor
        hidden = (gate / (1.0 + jnp.exp(-gate)) * up).astype(BF16)
        for n in range(PARTS):
            out_ref[n, :, pl.ds(at, tile)] = hidden


def finish_kernel(
    core_ref, mine_ref, near_ref, other_near_ref, far_ref, other_far_ref, middle_ref, out_ref
):
    result = middle_ref[...] + wide_total((core_ref, mine_ref, near_ref, other_near_ref, far_ref, other_far_ref))
    rows = out_ref.shape[1] // PARTS
    for n in range(PARTS):
        for m in range(2):
            at = (n * 2 + m) * rows
            out_ref[m, pl.ds(n * rows, rows), :] = result[at : at + rows, :]


def exchange(payload):
    return lax.all_to_all(payload, "narrow", 0, 0, tiled=True)


def move(sends, stage):
    taken = {}
    for step in (1, 3, 2):
        block = sends[step - 1].astype(F16)
        taken[step] = lax.ppermute(block, ("wide", "narrow"), plane_pairs(step, stage)).astype(F32)
    return [taken[step] for step in (1, 2, 3)]


def sum_wide_parts(partial, core_flag):
    rows, width = partial.shape
    half = rows // 2
    mine, part = call(
        total_kernel,
        [((rows, width), BF16), ((half, width), BF16)],
        4 * MIB,
        core_flag,
        partial,
        lax.ppermute(partial, "wide", CORE_SWAP),
        scalars=1,
    )
    near = lax.ppermute(mine, "wide", NEXT_Z)
    far = lax.ppermute(part, "wide", FAR_Z)
    other_near = lax.ppermute(near, "wide", CORE_SWAP)
    other_far = lax.ppermute(far, "wide", CORE_SWAP)
    return mine, near, other_near, far, other_far


def body(
    hidden_in,
    attn_gain,
    w_query,
    w_key,
    w_value,
    w_out,
    ffn_gain,
    w_gate,
    w_up,
    w_down,
    key_cache,
    value_cache,
    cache_len,
):
    micro, _, width = hidden_in.shape
    rows = key_cache.shape[1]
    here = micro * rows
    every = here * PARTS
    split = w_query.shape[1]
    units = w_gate.shape[1]
    core = lax.axis_index("wide") % 2
    at_y, at_x = lax.axis_index("narrow") // SIDE, lax.axis_index("narrow") % SIDE
    first, second = jnp.arange(PARTS) // SIDE, jnp.arange(PARTS) % SIDE
    step_y = jnp.where(core == 0, second, first)
    step_x = jnp.where(core == 0, first, second)
    blocks = ((at_y + step_y) % SIDE * SIDE + (at_x + step_x) % SIDE).astype(jnp.int32)
    core_flag = core.astype(jnp.int32)[None]

    base = 500000.0 ** (-np.arange(HEAD // 2) * 2.0 / HEAD)
    base = np.concatenate([base, base])[None].astype(np.float32)
    held = (here, key_cache.shape[3], HEAD)
    payload, stream, cosines, sines, lengths, keys, values = call(
        project_kernel,
        [((every, split + 3 * HEAD), F32), ((every, width), F32)]
        + [((here, HEAD), F32)] * 2
        + [((here, HEAD), jnp.int32)]
        + [(held, BF16)] * 2,
        8 * MIB,
        blocks,
        core_flag,
        cache_len,
        jnp.asarray(base),
        hidden_in,
        attn_gain[None],
        w_query,
        w_key,
        w_value,
        key_cache.reshape(held),
        value_cache.reshape(held),
        scalars=2,
        far=9,
        kept=2,
        scratch=[pltpu.SMEM(cache_len.shape, jnp.int32), pltpu.VMEM((1, HEAD), F32)]
        + [pltpu.VMEM(hidden_in.shape, F32), pltpu.VMEM((1, width), F32)]
        + [pltpu.VMEM(w.shape, BF16) for w in (w_query, w_key, w_value)]
        + [pltpu.SemaphoreType.DMA((7,))]
        + [pltpu.SemaphoreType.DMA((here, held[1] // 512))] * 2,
    )
    got = exchange(payload.astype(F16).reshape(PARTS, here, -1))
    last = split + 2 * HEAD
    norms = got[:, :, last : last + len(NORM_SCALES)].astype(F32)
    norms = jnp.sum(norms * (1.0 / jnp.array(NORM_SCALES, F32)), axis=-1, keepdims=True)
    total = jnp.sum(got[:, :, :last].astype(F32) * (norms * (1.0 / REACH)), axis=0)
    squares = jnp.sum(jnp.broadcast_to(norms * norms, (PARTS, here, LANES)), axis=0)

    (attended,) = call(
        attend_kernel,
        [((PARTS, here, split), BF16)],
        16 * MIB,
        lengths,
        total,
        squares,
        cosines,
        sines,
        keys,
        values,
        held=2,
        scratch=[pltpu.VMEM((here, split // HEAD, HEAD), F32)] * 2
        + [pltpu.VMEM((here * split // HEAD, held[1]), F32)],
    )
    gathered = exchange(attended).reshape(every, split)
    parts = sum_wide_parts(jnp.dot(gathered, w_out, preferred_element_type=F32), core_flag)
    group = every // SIDE
    full = 2 * units + LANES
    middle, own, *sends = call(
        gate_kernel,
        [((every, width), F32)] + [((group, full), F32)] * SIDE,
        8 * MIB,
        core_flag,
        blocks,
        *parts,
        stream,
        ffn_gain[None],
        w_gate,
        w_up,
        scalars=2,
        held=2,
        scratch=[pltpu.VMEM((every, width), F32), pltpu.VMEM((every, width), BF16)],
    )
    taken = move(sends, 0)
    own, *sends = call(middle_sum_kernel, [((here, full), F32)] * SIDE, 8 * MIB, own, *taken)
    taken = move(sends, 1)
    (hidden,) = call(hidden_kernel, [((PARTS, here, units), BF16)], 8 * MIB, own, *taken)
    gathered = exchange(hidden).reshape(every, units)
    parts = sum_wide_parts(jnp.dot(gathered, w_down, preferred_element_type=F32), core_flag)
    (result,) = call(
        finish_kernel, [(hidden_in.shape, F32)], 8 * MIB, core_flag, *parts, middle, scalars=1
    )
    return result


def solution(mesh):
    return jax.shard_map(
        body,
        mesh=mesh,
        in_specs=(
            P(None, None, "narrow"),
            P("narrow"),
            P("narrow", "wide"),
            P("narrow", "wide"),
            P("narrow", "wide"),
            P("wide", "narrow"),
            P("narrow"),
            P("narrow", "wide"),
            P("narrow", "wide"),
            P("wide", "narrow"),
            P(None, "narrow", "wide", None, None),
            P(None, "narrow", "wide", None, None),
            P(None, "narrow"),
        ),
        out_specs=P(None, None, "narrow"),
        check_vma=False,
    )
```

```python
import functools

import jax
import jax.numpy as jnp
import numpy as np
from jax import lax
from jax.experimental import pallas as pl
from jax.experimental.pallas import tpu as pltpu
from jax.sharding import PartitionSpec as P

D = 8192
EPSILON = 1e-05
BF16 = jnp.bfloat16
F16 = jnp.float16
F32 = jnp.float32
SIDE = 4
PARTS = SIDE * SIDE
HEAD = 128
LANES = 128
VMEM = pl.BlockSpec(memory_space=pltpu.VMEM)
HBM = pl.BlockSpec(memory_space=pltpu.HBM)
SMEM = pl.BlockSpec(memory_space=pltpu.SMEM)
KIB = 1 << 10
MIB = 1 << 20
REACH = 8192.0
NORM_SCALES = (2.0**-2, 2.0**6, 2.0**16)


def wide_pairs(target):
    pairs = []
    for z in range(SIDE):
        for c in range(2):
            to_z, to_c = target(z, c)
            pairs.append((z * 2 + c, to_z % SIDE * 2 + to_c))
    return pairs


CORE_SWAP = wide_pairs(lambda z, c: (z, 1 - c))
NEXT_Z = wide_pairs(lambda z, c: (z + 1 if c == 0 else z - 1, c))
FAR_Z = wide_pairs(lambda z, c: (z + 2, c))


def plane_pairs(step, stage):
    pairs = []
    for w in range(2 * SIDE):
        for y in range(SIDE):
            for x in range(SIDE):
                along_x = (w % 2 == 0) == (stage == 0)
                to_y, to_x = (y, (x + step) % SIDE) if along_x else ((y + step) % SIDE, x)
                pairs.append((w * PARTS + y * SIDE + x, w * PARTS + to_y * SIDE + to_x))
    return pairs


def call(kernel, outs, limit, *operands, scratch=(), scalars=0, far=0, held=0, kept=0):
    near = len(operands) - far
    specs = [SMEM] * scalars + [VMEM] * (near - scalars) + [HBM] * far
    size = sum(o.size * o.dtype.itemsize for o in operands)
    places = [None] * (near - held) + [pltpu.VMEM] * held + [pltpu.HBM] * far
    operands = [
        o if place is None else pltpu.with_memory_space_constraint(o, place)
        for o, place in zip(operands, places)
    ]
    return pl.pallas_call(
        kernel,
        out_shape=[
            (jax.ShapeDtypeStruct if i < len(outs) - kept else pltpu.VMEM)(shape, kind)
            for i, (shape, kind) in enumerate(outs)
        ],
        in_specs=specs,
        out_specs=[VMEM] * len(outs),
        scratch_shapes=scratch,
        compiler_params=pltpu.CompilerParams(vmem_limit_bytes=limit),
        cost_estimate=pl.CostEstimate(flops=0, bytes_accessed=size, transcendentals=0),
    )(*operands)


def reach(squares):
    return REACH * lax.rsqrt(jnp.maximum(squares, 1e-30))


def write_norm(squares):
    rest = squares * lax.rsqrt(jnp.maximum(squares, 1e-30))
    lane = lax.broadcasted_iota(jnp.int32, (squares.shape[0], LANES), 1)
    tile = jnp.zeros((squares.shape[0], LANES), F32)
    for i, factor in enumerate(NORM_SCALES):
        part = rest * factor
        if i < 2:
            part = part.astype(BF16).astype(F32)
            part = jnp.where(jnp.abs(part) < 2.0**-10, 0.0, part)
        rest = rest - part * (1.0 / factor)
        tile = jnp.where(lane == i, part, tile)
    return tile


def read_norm(tile):
    parts = [tile[:, i : i + 1] * (1.0 / factor) for i, factor in enumerate(NORM_SCALES)]
    return (parts[0] + parts[1]) + parts[2]


def weighted(refs):
    last = refs[0].shape[1] - LANES
    norms = [read_norm(ref[:, pl.ds(last, LANES)]) for ref in refs]
    squares = [norm * norm for norm in norms]
    weights = [norm * (1.0 / REACH) for norm in norms]

    def total(at, size):
        parts = [ref[:, pl.ds(at, size)] * weight for ref, weight in zip(refs, weights)]
        return (parts[0] + parts[1]) + (parts[2] + parts[3])

    return total, (squares[0] + squares[1]) + (squares[2] + squares[3])


def project_kernel(
    blocks_ref, core_ref, len_hbm, base_hbm, x_hbm, gain_hbm, wq_hbm, wk_hbm, wv_hbm, keys_hbm, values_hbm,
    out_ref, stream_ref, cos_ref, sin_ref, lengths_ref, keys_s, values_s, len_s, base_ref, x_ref, gain_ref,
    wq_ref, wk_ref, wv_ref, sems, key_sems, value_sems,
):
    pairs = ((x_hbm, x_ref), (gain_hbm, gain_ref), (wq_hbm, wq_ref), (wk_hbm, wk_ref), (wv_hbm, wv_ref))
    copies = [pltpu.make_async_copy(a, b, sems.at[i]) for i, (a, b) in enumerate(pairs)]
    first = pltpu.make_async_copy(len_hbm, len_s, sems.at[5])
    table = pltpu.make_async_copy(base_hbm, base_ref, sems.at[6])
    for copy in (first, *copies, table):
        copy.start()
    first.wait()
    local = len_s.shape[1]
    len_ref = [len_s[r // local, r % local] for r in range(keys_s.shape[0])]
    chunk = 256
    here, cache = keys_s.shape[0], keys_s.shape[1]
    counts = [lax.shift_right_logical(len_ref[r] + (chunk - 1), 8) for r in range(here)]

    def fetch(far, near, sems, r, j):
        part = pl.ds(pl.multiple_of(j * chunk, chunk), chunk)
        return pltpu.make_async_copy(far.at[r, part], near.at[r, part], sems.at[r, j])

    def start(far, near, sems, r):
        @pl.loop(0, counts[r])
        def _(j):
            fetch(far, near, sems, r, j).start()

    def finish(far, near, sems, r):
        @pl.loop(0, counts[r])
        def _(j):
            fetch(far, near, sems, r, j).wait()

    for r in range(here):
        start(keys_hbm, keys_s, key_sems, r)
    for r in range(here):
        start(values_hbm, values_s, value_sems, r)
    for r in range(here):

        @pl.loop(counts[r], cache // chunk)
        def _(j):
            part = pl.ds(pl.multiple_of(j * chunk, chunk), chunk)
            values_s[r, part, :] = jnp.zeros((chunk, HEAD), BF16)
    row = lax.broadcasted_iota(jnp.int32, lengths_ref.shape, 0)
    lengths = jnp.zeros(lengths_ref.shape, jnp.int32)
    for r in range(here):
        lengths = jnp.where(row == r, len_ref[r], lengths)
    lengths_ref[...] = lengths
    table.wait()
    angles = lengths.astype(F32) * base_ref[...]
    lane = lax.broadcasted_iota(jnp.int32, lengths_ref.shape, 1)
    cos_ref[...] = jnp.cos(angles)
    sines = jnp.sin(angles)
    sin_ref[...] = jnp.where(lane < HEAD // 2, -sines, sines)
    copies[0].wait()
    copies[1].wait()
    rows = x_ref.shape[1] // PARTS
    for n in range(PARTS):
        for m in range(2):
            stream_ref[pl.ds((n * 2 + m) * rows, rows), :] = x_ref[m, pl.ds(n * rows, rows), :]
    stream = stream_ref[...]
    squares = jnp.sum(stream * stream, axis=-1, keepdims=True)
    scale = reach(squares)
    normed = (stream * gain_ref[...]).astype(BF16)
    at = 0
    for copy, w_ref in zip(copies[2:], (wq_ref, wk_ref, wv_ref)):
        copy.wait()
        width = w_ref.shape[1]
        product = jnp.dot(normed, w_ref[...], preferred_element_type=F32)
        out_ref[:, pl.ds(at, width)] = product * scale
        at += width
    out_ref[:, pl.ds(at, LANES)] = write_norm(squares)
    for r in range(here):
        finish(keys_hbm, keys_s, key_sems, r)
        finish(values_hbm, values_s, value_sems, r)


def total_kernel(core_ref, mine_ref, other_ref, total_ref, half_ref):
    total = (mine_ref[...].astype(F32) + other_ref[...].astype(F32)).astype(BF16)
    total_ref[...] = total
    half = half_ref.shape[0]
    half_ref[...] = jnp.where(core_ref[0] == 0, total[:half, :], total[half:, :])


def attend_kernel(
    lengths_ref, total_ref, squares_ref, cos_ref, sin_ref, keys_ref, values_ref, out_ref, q_s, a_s, s_s,
):
    here = total_ref.shape[0]
    cache = keys_ref.shape[1]
    total = total_ref[...]
    heads = out_ref.shape[2] // HEAD
    split = heads * HEAD
    factor = lax.rsqrt(squares_ref[:, 0:1] / D + EPSILON)
    cos, sin = cos_ref[...], sin_ref[...]

    def turned(part):
        part = part * factor
        return (part * cos + pltpu.roll(part, HEAD // 2, 1) * sin).astype(BF16).astype(F32)

    key_new = turned(total[:, split : split + HEAD])
    value_new = (total[:, split + HEAD :] * factor).astype(BF16).astype(F32)
    for h in range(heads):
        q_s[:, h, :] = turned(total[:, h * HEAD : (h + 1) * HEAD])
    scaling = HEAD ** (-0.5)
    position = lax.broadcasted_iota(jnp.int32, (1, cache), 1)
    own = []
    for r in range(here):
        queries = q_s[r]
        scores = lax.dot_general(
            queries.astype(BF16),
            keys_ref[r],
            (((1,), (1,)), ((), ())),
            preferred_element_type=F32,
        )
        s_s[pl.ds(r * heads, heads), :] = jnp.where(
            position < lengths_ref[pl.ds(r, 1), pl.ds(0, 1)], scores * scaling, -jnp.inf
        )
        own.append(jnp.sum(queries * key_new[r : r + 1, :], axis=-1, keepdims=True) * scaling)
    weights, own_weights = [], []
    for r in range(here):
        scores = s_s[pl.ds(r * heads, heads), :]
        highest = jnp.maximum(jnp.max(scores, axis=-1, keepdims=True), own[r])
        shifted = jnp.exp(scores - highest)
        own_term = jnp.exp(own[r] - highest)
        totals = jnp.sum(shifted, axis=-1, keepdims=True) + own_term
        weights.append((shifted / totals).astype(BF16))
        own_weights.append((own_term / totals).astype(BF16).astype(F32))
    for r in range(here):
        attended = jnp.dot(weights[r], values_ref[r], preferred_element_type=F32)
        a_s[r] = attended + own_weights[r] * value_new[r : r + 1, :]
    for h in range(heads):
        part = a_s[:, h, :].astype(BF16)
        for n in range(PARTS):
            out_ref[n, :, pl.ds(h * HEAD, HEAD)] = part


def wide_total(refs):
    core_ref, mine_ref, near_ref, other_near_ref, far_ref, other_far_ref = refs
    first = core_ref[0] == 0
    far, far_other = far_ref[...].astype(F32), other_far_ref[...].astype(F32)
    opposite = jnp.concatenate(
        [jnp.where(first, far, far_other), jnp.where(first, far_other, far)], axis=0
    )
    sides = near_ref[...].astype(F32) + other_near_ref[...].astype(F32)
    return (mine_ref[...].astype(F32) + opposite) + sides


def gate_kernel(
    core_ref, blocks_ref, mine_ref, near_ref, other_near_ref, far_ref, other_far_ref, stream_ref, gain_ref,
    wg_ref, wu_ref, middle_ref, out0_ref, out1_ref, out2_ref, out3_ref, sorted_s, normed_s,
):
    middle_ref[...] = stream_ref[...] + wide_total(
        (core_ref, mine_ref, near_ref, other_near_ref, far_ref, other_far_ref)
    )
    rows = middle_ref.shape[0] // PARTS
    for i in range(PARTS):
        start = pl.multiple_of(blocks_ref[i] * rows, rows)
        sorted_s[pl.ds(i * rows, rows), :] = middle_ref[pl.ds(start, rows), :]
    middle = sorted_s[...]
    squares = jnp.sum(middle * middle, axis=-1, keepdims=True)
    scale, norm = reach(squares), write_norm(squares)
    normed_s[...] = (middle * gain_ref[...]).astype(BF16)
    outs = (out0_ref, out1_ref, out2_ref, out3_ref)
    units = wg_ref.shape[1]
    group = middle.shape[0] // SIDE
    tile = 512
    normed = normed_s[...]
    for at, w_ref in ((0, wg_ref), (units, wu_ref)):
        for j in range(0, units, tile):
            product = jnp.dot(normed, w_ref[:, pl.ds(j, tile)], preferred_element_type=F32) * scale
            for d in range(SIDE):
                outs[d][:, pl.ds(at + j, tile)] = product[d * group : (d + 1) * group, :]
    for d in range(SIDE):
        outs[d][:, pl.ds(2 * units, LANES)] = norm[d * group : (d + 1) * group, :]


def middle_sum_kernel(a_ref, b_ref, c_ref, d_ref, out0_ref, out1_ref, out2_ref, out3_ref):
    last = a_ref.shape[1] - LANES
    tile = 1024
    rows = a_ref.shape[0] // SIDE
    total, squares = weighted((a_ref, b_ref, c_ref, d_ref))
    scale = reach(squares)
    outs = (out0_ref, out1_ref, out2_ref, out3_ref)

    def put(at, size, value):
        for k in range(SIDE):
            outs[k][:, pl.ds(at, size)] = value[k * rows : (k + 1) * rows, :]

    for at in range(0, last, tile):
        put(at, tile, total(at, tile) * scale)
    put(last, LANES, write_norm(squares))


def hidden_kernel(a_ref, b_ref, c_ref, d_ref, out_ref):
    units = out_ref.shape[2]
    tile = 512
    total, squares = weighted((a_ref, b_ref, c_ref, d_ref))
    factor = lax.rsqrt(squares / D + EPSILON)
    for at in range(0, units, tile):
        gate = total(at, tile) * factor
        up = total(units + at, tile) * factor
        hidden = (gate / (1.0 + jnp.exp(-gate)) * up).astype(BF16)
        for n in range(PARTS):
            out_ref[n, :, pl.ds(at, tile)] = hidden


def finish_kernel(
    core_ref, mine_ref, near_ref, other_near_ref, far_ref, other_far_ref, middle_ref, out_ref
):
    result = middle_ref[...] + wide_total((core_ref, mine_ref, near_ref, other_near_ref, far_ref, other_far_ref))
    rows = out_ref.shape[1] // PARTS
    for n in range(PARTS):
        for m in range(2):
            at = (n * 2 + m) * rows
            out_ref[m, pl.ds(n * rows, rows), :] = result[at : at + rows, :]


def exchange(payload):
    return lax.all_to_all(payload, "narrow", 0, 0, tiled=True)


def move(sends, stage):
    taken = {}
    for step in (1, 3, 2):
        block = sends[step - 1].astype(F16)
        taken[step] = lax.ppermute(block, ("wide", "narrow"), plane_pairs(step, stage)).astype(F32)
    return [taken[step] for step in (1, 2, 3)]


def sum_wide_parts(partial, core_flag):
    rows, width = partial.shape
    half = rows // 2
    mine, part = call(
        total_kernel,
        [((rows, width), BF16), ((half, width), BF16)],
        4 * MIB,
        core_flag,
        partial,
        lax.ppermute(partial, "wide", CORE_SWAP),
        scalars=1,
    )
    near = lax.ppermute(mine, "wide", NEXT_Z)
    far = lax.ppermute(part, "wide", FAR_Z)
    other_near = lax.ppermute(near, "wide", CORE_SWAP)
    other_far = lax.ppermute(far, "wide", CORE_SWAP)
    return mine, near, other_near, far, other_far


def body(
    hidden_in,
    attn_gain,
    w_query,
    w_key,
    w_value,
    w_out,
    ffn_gain,
    w_gate,
    w_up,
    w_down,
    key_cache,
    value_cache,
    cache_len,
):
    micro, _, width = hidden_in.shape
    rows = key_cache.shape[1]
    here = micro * rows
    every = here * PARTS
    split = w_query.shape[1]
    units = w_gate.shape[1]
    core = lax.axis_index("wide") % 2
    at_y, at_x = lax.axis_index("narrow") // SIDE, lax.axis_index("narrow") % SIDE
    first, second = jnp.arange(PARTS) // SIDE, jnp.arange(PARTS) % SIDE
    step_y = jnp.where(core == 0, second, first)
    step_x = jnp.where(core == 0, first, second)
    blocks = ((at_y + step_y) % SIDE * SIDE + (at_x + step_x) % SIDE).astype(jnp.int32)
    core_flag = core.astype(jnp.int32)[None]

    base = 500000.0 ** (-np.arange(HEAD // 2) * 2.0 / HEAD)
    base = np.concatenate([base, base])[None].astype(np.float32)
    held = (here, key_cache.shape[3], HEAD)
    payload, stream, cosines, sines, lengths, keys, values = call(
        project_kernel,
        [((every, split + 3 * HEAD), F32), ((every, width), F32)]
        + [((here, HEAD), F32)] * 2
        + [((here, HEAD), jnp.int32)]
        + [(held, BF16)] * 2,
        8 * MIB,
        blocks,
        core_flag,
        cache_len,
        jnp.asarray(base),
        hidden_in,
        attn_gain[None],
        w_query,
        w_key,
        w_value,
        key_cache.reshape(held),
        value_cache.reshape(held),
        scalars=2,
        far=9,
        kept=2,
        scratch=[pltpu.SMEM(cache_len.shape, jnp.int32), pltpu.VMEM((1, HEAD), F32)]
        + [pltpu.VMEM(hidden_in.shape, F32), pltpu.VMEM((1, width), F32)]
        + [pltpu.VMEM(w.shape, BF16) for w in (w_query, w_key, w_value)]
        + [pltpu.SemaphoreType.DMA((7,))]
        + [pltpu.SemaphoreType.DMA((here, held[1] // 256))] * 2,
    )
    got = exchange(payload.astype(F16).reshape(PARTS, here, -1))
    last = split + 2 * HEAD
    norms = got[:, :, last : last + len(NORM_SCALES)].astype(F32)
    norms = jnp.sum(norms * (1.0 / jnp.array(NORM_SCALES, F32)), axis=-1, keepdims=True)
    total = jnp.sum(got[:, :, :last].astype(F32) * (norms * (1.0 / REACH)), axis=0)
    squares = jnp.sum(jnp.broadcast_to(norms * norms, (PARTS, here, LANES)), axis=0)

    (attended,) = call(
        attend_kernel,
        [((PARTS, here, split), BF16)],
        16 * MIB,
        lengths,
        total,
        squares,
        cosines,
        sines,
        keys,
        values,
        held=2,
        scratch=[pltpu.VMEM((here, split // HEAD, HEAD), F32)] * 2
        + [pltpu.VMEM((here * split // HEAD, held[1]), F32)],
    )
    gathered = exchange(attended).reshape(every, split)
    parts = sum_wide_parts(jnp.dot(gathered, w_out, preferred_element_type=F32), core_flag)
    group = every // SIDE
    full = 2 * units + LANES
    middle, own, *sends = call(
        gate_kernel,
        [((every, width), F32)] + [((group, full), F32)] * SIDE,
        8 * MIB,
        core_flag,
        blocks,
        *parts,
        stream,
        ffn_gain[None],
        w_gate,
        w_up,
        scalars=2,
        held=2,
        scratch=[pltpu.VMEM((every, width), F32), pltpu.VMEM((every, width), BF16)],
    )
    taken = move(sends, 0)
    own, *sends = call(middle_sum_kernel, [((here, full), F32)] * SIDE, 8 * MIB, own, *taken)
    taken = move(sends, 1)
    (hidden,) = call(hidden_kernel, [((PARTS, here, units), BF16)], 8 * MIB, own, *taken)
    gathered = exchange(hidden).reshape(every, units)
    parts = sum_wide_parts(
        jnp.dot(gathered, w_down, preferred_element_type=F32).astype(BF16), core_flag
    )
    (result,) = call(
        finish_kernel, [(hidden_in.shape, F32)], 8 * MIB, core_flag, *parts, middle, scalars=1
    )
    return result


def solution(mesh):
    return jax.shard_map(
        body,
        mesh=mesh,
        in_specs=(
            P(None, None, "narrow"),
            P("narrow"),
            P("narrow", "wide"),
            P("narrow", "wide"),
            P("narrow", "wide"),
            P("wide", "narrow"),
            P("narrow"),
            P("narrow", "wide"),
            P("narrow", "wide"),
            P("wide", "narrow"),
            P(None, "narrow", "wide", None, None),
            P(None, "narrow", "wide", None, None),
            P(None, "narrow"),
        ),
        out_specs=P(None, None, "narrow"),
        check_vma=False,
    )
```
